32 devices in a mesh: date: 4 (over y, core), tile: 8 (over z, x).
Axes of the slice: x: 2, y: 2, z: 4, core: 2. Of those that a mesh axis runs over, the one named last changes fastest.
Arguments:
- granules: bfloat16 [16, 10, 640, 512], P('date', None, 'tile'), may hold values from -6 to 6
- coef_x: bfloat16 [8, 5, 128, 12], P('tile'), may hold values from -1.75 to 1.75
- coef_y: bfloat16 [8, 5, 16, 12], P('tile'), may hold values from -1.75 to 1.75
- row_offset: int32 [8, 5], P('tile'), may hold values from 0 to 36
- col_offset: int32 [8, 5], P('tile'), may hold values from 0 to 244
- targets: int32 [8, 5], P('tile'), may hold values from -1 to 7, as said below
- mask: int32 [16, 8], P(None, 'tile'), may hold values from 0 to 1, as said below
- smoother: float32 [16, 16], replicated, as said below
Outputs:
- smoothed: float32 [16, 10, 8, 2048], P(None, None, 'tile', 'date')
The draws below stay inside these ranges and needn't reach their ends.
Inputs may be any that keep to these rules, and one draw needn't show every extreme that they name: `targets`: slot 0 of granule g names tile g; the other slots name, in an order drawn from the seed, each tile other than g within 2 of g in index once, and -1 where such a tile lies beyond the ends. `mask`: every tile has at least one valid date. `smoother`: every entry is positive.
All inputs are finite; a program needn't handle non-finite values.
Results may differ from the reference program's by a relative error of at most 0.0004.
Values sent between devices are 32-bit elements; how exact they have to be, the bound alone decides.
A program may use at most 128 MiB of HBM per device.

```python
import jax
import jax.numpy as jnp
from jax import lax

BANDS = 10
TAPS = 12
RADIUS = 2
KMAX = 5
TR = 16
TC = 128
GR = 80
GC = 512
TILES = 8
DATES = 16


def draw_targets(key, part):
    key = jax.random.fold_in(key, 11)
    order_keys = jax.random.split(key, TILES)
    orders = jax.vmap(lambda single: jax.random.permutation(single, 2 * RADIUS))(order_keys)
    candidates = jnp.concatenate([jnp.arange(-RADIUS, 0, dtype=jnp.int32), jnp.arange(1, RADIUS + 1, dtype=jnp.int32)])
    reaches = candidates[orders]
    own_tile = jnp.arange(TILES, dtype=jnp.int32)[:, None]
    aimed = own_tile + reaches
    usable = (aimed >= 0) & (aimed < TILES)
    return jnp.concatenate([own_tile, jnp.where(usable, aimed, -1)], 1).astype(jnp.int32)


def draw_mask(key, part):
    key = jax.random.fold_in(key, 12)
    flag_key, pick_key = jax.random.split(key)
    flags = (jax.random.randint(flag_key, (DATES, TILES), 0, 10) < 7).astype(jnp.int32)
    picked = jax.random.randint(pick_key, (1, TILES), 0, DATES)
    forced = (jnp.arange(DATES, dtype=jnp.int32)[:, None] == picked).astype(jnp.int32)
    return jnp.maximum(flags, forced).astype(jnp.int32)


def draw_smoother(key, part):
    key = jax.random.fold_in(key, 13)
    places = jnp.arange(DATES, dtype=jnp.float32)
    gaps = jnp.abs(places[:, None] - places[None, :])
    decay = jnp.exp(-4.0 * gaps / DATES)
    factor = jax.random.uniform(key, (DATES, DATES), jnp.float32, 0.5, 1.5)
    return (decay * factor).astype(jnp.float32)


def plant(result, rng, low, high):
    index_at = [jax.random.randint(jax.random.fold_in(rng, axis), (), 0, length) for axis, length in enumerate(result.shape)]
    main_axis = result.shape.index(max(result.shape))
    next_to = index_at[:main_axis] + [(index_at[main_axis] + 1) % result.shape[main_axis]] + index_at[main_axis + 1:]
    return result.at[tuple(index_at)].set(low).at[tuple(next_to)].set(high)


def level_of(stream_key, extent, pieces, least, top_value):
    factor_of, own = 1.0, jax.random.fold_in(stream_key, 6)
    for position, parts in pieces:
        draws = jnp.exp(jax.random.uniform(jax.random.fold_in(own, position), (parts,), jnp.float32, least / len(pieces), top_value / len(pieces)))
        factor_of = factor_of * jnp.repeat(draws, extent[position] // parts).reshape([-1 if axis == position else 1 for axis in range(len(extent))])
    return factor_of


def bell_draw(key, shape, spread, bound, cuts=(), kind=jnp.bfloat16):
    factor_of = level_of(key, shape, cuts, -0.22, 0.18) if cuts else 1.0
    result = jax.random.normal(key, shape, jnp.float32) * spread * factor_of
    return jnp.minimum(jnp.maximum(result, -bound), bound).astype(kind)


def setup_inputs(seed: int = 0) -> dict:
    key_of = jax.random.split(jax.random.key(seed), 9)
    granules = bell_draw(key_of[0], (DATES, BANDS, TILES * GR, GC), 1.0, 6.0, ((0, 4), (2, 8)))
    coef_x = bell_draw(key_of[1], (TILES, KMAX, TC, TAPS), TAPS ** -0.5, 1.75, ((0, 8),))
    coef_y = bell_draw(key_of[2], (TILES, KMAX, TR, TAPS), TAPS ** -0.5, 1.75, ((0, 8),))
    row_offset = plant(jax.random.randint(key_of[3], (TILES, KMAX), 0, GR - 2 * TR - TAPS + 1), jax.random.fold_in(key_of[3], 1), 0, GR - 2 * TR - TAPS).astype(jnp.int32)
    col_offset = plant(jax.random.randint(key_of[4], (TILES, KMAX), 0, GC - 2 * TC - TAPS + 1), jax.random.fold_in(key_of[4], 1), 0, GC - 2 * TC - TAPS).astype(jnp.int32)
    targets = draw_targets(jax.random.fold_in(key_of[8], 71), 0)
    mask = draw_mask(jax.random.fold_in(key_of[8], 71), 0)
    smoother = draw_smoother(jax.random.fold_in(key_of[8], 71), 0)
    return dict(granules=granules, coef_x=coef_x, coef_y=coef_y, row_offset=row_offset, col_offset=col_offset, targets=targets, mask=mask, smoother=smoother)


def band_matrix(coeffs, offset, span_width):
    row_count = coeffs.shape[0]
    row_ids = jnp.arange(row_count, dtype=jnp.int32)[:, None]
    col_ids = jnp.arange(span_width, dtype=jnp.int32)[None, :]
    tap_index = col_ids - 2 * row_ids - offset.astype(jnp.int32)
    banded = jnp.zeros((row_count, span_width), jnp.float32)
    for tap_number in range(coeffs.shape[1]):
        picked = coeffs[:, tap_number:tap_number + 1].astype(jnp.float32)
        banded = banded + jnp.where(tap_index == tap_number, picked, jnp.float32(0.0))
    return banded


def resample(granule, x_coeffs, y_coeffs, row_shift, col_shift):
    slot_count = x_coeffs.shape[0]
    tile_cols = x_coeffs.shape[1]
    dates_here, band_count, grid_rows, grid_cols = granule.shape
    x_mats = jnp.concatenate([band_matrix(x_coeffs[slot], col_shift[slot], grid_cols) for slot in range(slot_count)], 0).astype(jnp.bfloat16)
    x_pass = jnp.dot(granule.reshape(-1, grid_cols), x_mats.T, preferred_element_type=jnp.float32)
    x_pass = x_pass.reshape(dates_here, band_count, grid_rows, slot_count, tile_cols)
    y_mats = jnp.stack([band_matrix(y_coeffs[slot], row_shift[slot], grid_rows) for slot in range(slot_count)], 0)
    return jnp.einsum("kir,dbrkj->kdbij", y_mats, x_pass, precision=lax.Precision.HIGHEST)


def reference(granules, coef_x, coef_y, row_offset, col_offset, targets, mask, smoother):
    def visit(tile_sums, inputs):
        granule_id, x_coeffs, y_coeffs, row_shift, col_shift, aimed = inputs
        granule = lax.dynamic_slice_in_dim(granules, granule_id * GR, GR, 2)
        partials = resample(granule, x_coeffs, y_coeffs, row_shift, col_shift)
        chosen = (aimed[:, None] == jnp.arange(TILES, dtype=jnp.int32)[None, :]).astype(jnp.float32)
        added = jnp.einsum("kt,kdbij->tdbij", chosen, partials, precision=lax.Precision.HIGHEST)
        return tile_sums + added, granule_id

    start_sums = jnp.zeros((TILES, DATES, BANDS, TR, TC), jnp.float32)
    tile_sums, ignored = lax.scan(visit, start_sums, (jnp.arange(TILES, dtype=jnp.int32), coef_x, coef_y, row_offset, col_offset, targets))
    series = tile_sums.reshape(TILES, DATES, BANDS, TR * TC)
    valid = mask.astype(jnp.float32)
    weighted = series * jnp.transpose(valid)[:, :, None, None]
    numerator = jnp.einsum("ts,usbp->tbup", smoother, weighted, precision=lax.Precision.HIGHEST)
    denominator = jnp.dot(smoother, valid, precision=lax.Precision.HIGHEST)
    return numerator / denominator[:, None, :, None]
```

```python
import functools

import jax
import jax.numpy as jnp
from jax import lax
from jax.experimental import pallas as pl
from jax.experimental.pallas import tpu as pltpu
from jax.sharding import PartitionSpec as P

RADIUS = 2
MESH = pl.DeviceIdType.MESH
ROWS = 64


def kernel(dims, tgt, roff, coff, mask, smoother, cx_ref, cy_ref, g_hbm, out_ref,
           g, rx, ymat, high, low, part, recv, final,
           g_sem, send1, recv1, send2, recv2):
    nt, nq, slots, tile_rows, tile_cols, taps, grid_rows, grid_cols, group, rpq, steps, all_dates, bands = dims
    reaches = list(range(-RADIUS, RADIUS + 1))
    home = RADIUS
    others = [0, 4, 1, 3]
    tile = lax.axis_index("tile")
    date = lax.axis_index("date")

    def fetch(step):
        return pltpu.make_async_copy(g_hbm.at[pl.ds(2 * step, 2)], g.at[pl.ds(2 * step, 2)], g_sem.at[step])

    for step in range(steps):
        fetch(step).start()

    def inside(place):
        return jnp.logical_and(place >= 0, place < nt)

    barrier = pltpu.get_barrier_semaphore()
    for ri in others:
        there = tile + reaches[ri]

        @pl.when(inside(there))
        def _(there=there):
            pl.semaphore_signal(barrier, inc=1, device_id=(date, there), device_id_type=MESH)

    for c in range(1, nq):
        pl.semaphore_signal(barrier, inc=1, device_id=(lax.rem(date + c, nq), tile), device_id_type=MESH)

    m_count, c_count = slots * tile_rows * group, group * grid_rows
    per_slot = tile_rows * group
    m_e = lax.broadcasted_iota(jnp.int32, (m_count, slots * tile_rows), 0)
    n_e = lax.broadcasted_iota(jnp.int32, (m_count, slots * tile_rows), 1)

    def row_of(m):
        return ((m % per_slot) // (group * rpq)) * rpq + m % rpq

    aimed = jnp.full_like(n_e, -1)
    for k in range(slots):
        aimed = jnp.where(n_e // tile_rows == k, tgt[0, k], aimed)
    wanted = m_e // per_slot + (tile - RADIUS)
    pick = jnp.where(jnp.logical_and(row_of(m_e) == n_e % tile_rows, aimed == wanted), 1.0, 0.0)
    cy = jnp.dot(pick.astype(jnp.bfloat16), cy_ref[...], preferred_element_type=jnp.float32)
    m = lax.broadcasted_iota(jnp.int32, (m_count, c_count), 0)
    c = lax.broadcasted_iota(jnp.int32, (m_count, c_count), 1)
    shift = jnp.zeros_like(m)
    reach_tile = m // per_slot + (tile - RADIUS)
    for k in range(slots):
        shift = jnp.where(reach_tile == tgt[0, k], roff[0, k], shift)
    band_c = jnp.zeros_like(c)
    for b in range(1, group):
        band_c = jnp.where(c >= b * grid_rows, b, band_c)
    tap = c - band_c * grid_rows - 2 * row_of(m) - shift
    tap = jnp.where((m // rpq) % group == band_c, tap, -1)
    acc = jnp.zeros((m_count, c_count), jnp.float32)
    for t in range(taps):
        acc = jnp.where(tap == t, cy[:, t:t + 1], acc)
    ymat[...] = acc.astype(jnp.bfloat16)

    def build(r, carry):
        want = tile + (r - RADIUS)
        coef = jnp.zeros((taps, tile_cols), jnp.float32)
        off = jnp.int32(0)
        for k in range(slots):
            hit = tgt[0, k] == want
            coef = coef + cx_ref[k].astype(jnp.float32) * jnp.where(hit, 1.0, 0.0)
            off = off + jnp.where(hit, coff[0, k], 0)
        row = lax.broadcasted_iota(jnp.int32, (ROWS, tile_cols), 0)
        lane = lax.broadcasted_iota(jnp.int32, (ROWS, tile_cols), 1)
        base = row - 2 * lane - off
        for j in range(grid_cols // ROWS):
            tap = base + j * ROWS
            acc = jnp.zeros((ROWS, tile_cols), jnp.float32)
            for t in range(taps):
                acc = jnp.where(tap == t, coef[t:t + 1, :], acc)
            rx[r, j * ROWS:(j + 1) * ROWS, :] = acc.astype(jnp.bfloat16)
        return carry

    lax.fori_loop(0, slots, build, 0)

    for step in range(steps):
        fetch(step).wait()
        pair = [
            jnp.dot(ymat[...], g[2 * step + h], preferred_element_type=jnp.float32).reshape(slots * nq, 1, 8, grid_cols)
            for h in range(2)
        ]
        both = jnp.concatenate(pair, 1).reshape(slots, nq, 16, grid_cols)
        top = both.astype(jnp.bfloat16)
        high[:, :, step * 16:(step + 1) * 16, :] = top
        low[:, :, step * 16:(step + 1) * 16, :] = (both - top.astype(jnp.float32)).astype(jnp.bfloat16)

    peers = jnp.int32(nq - 1)
    for ri in others:
        peers = peers + jnp.where(inside(tile + reaches[ri]), 1, 0)
    pl.semaphore_wait(barrier, peers)

    def to_tile(ri, q):
        return pltpu.make_async_remote_copy(
            src_ref=part.at[ri, q], dst_ref=recv.at[ri, q], send_sem=send1.at[ri, q], recv_sem=recv1.at[ri, q],
            device_id=(date, tile + reaches[ri]), device_id_type=MESH)

    def to_date(q):
        return pltpu.make_async_remote_copy(
            src_ref=part.at[home, q], dst_ref=final.at[date], send_sem=send2.at[q], recv_sem=recv2.at[date],
            device_id=(q, tile), device_id_type=MESH)

    def from_date(q):
        return pltpu.make_async_remote_copy(
            src_ref=part.at[home, q], dst_ref=final.at[q], send_sem=send2.at[q], recv_sem=recv2.at[q],
            device_id=(q, tile), device_id_type=MESH)

    order = [nq // 2] + [s for s in range(1, nq) if s != nq // 2] + [0]
    blocks = [lax.rem(date + s, nq) for s in order]
    for q in blocks:
        for ri in others + [home]:
            part[ri, q] = (
                jnp.dot(high[ri, q], rx[ri], preferred_element_type=jnp.float32)
                + jnp.dot(low[ri, q], rx[ri], preferred_element_type=jnp.float32))
            if ri != home:

                @pl.when(inside(tile + reaches[ri]))
                def _(ri=ri, q=q):
                    to_tile(ri, q).start()

    for s, q in zip(order, blocks):
        for ri in others:

            @pl.when(inside(tile - reaches[ri]))
            def _(ri=ri, q=q):
                to_tile(ri, q).wait_recv()
                part[home, q] = part[home, q] + recv[ri, q]

        if s != 0:
            to_date(q).start()
        else:
            final[date] = part[home, q]

    for s, q in zip(order, blocks):
        if s != 0:
            from_date(q).wait_recv()

    rows = bands * rpq
    here = all_dates // nq
    valid = [mask[0, s].astype(jnp.float32) for s in range(all_dates)]

    def smooth(t, carry):
        total = jnp.zeros((rows, tile_cols), jnp.float32)
        weight = jnp.float32(0.0)
        for s in range(all_dates):
            w = smoother[t, s] * valid[s]
            weight = weight + w
            first = (s % here) * rows
            total = total + final[s // here, first:first + rows, :] * w
        out_ref[t] = total / jnp.full((rows, tile_cols), weight, jnp.float32)
        return carry

    lax.fori_loop(0, all_dates, smooth, 0)

    for s, q in zip(order, blocks):
        for ri in others:

            @pl.when(inside(tile + reaches[ri]))
            def _(ri=ri, q=q):
                to_tile(ri, q).wait_send()

        if s != 0:
            to_date(q).wait_send()


def body(granules, coef_x, coef_y, row_offset, col_offset, targets, mask, smoother):
    dates, bands, grid_rows, grid_cols = granules.shape
    _, slots, tile_cols, taps = coef_x.shape
    tile_rows = coef_y.shape[2]
    nq, nt = lax.axis_size("date"), lax.axis_size("tile")
    rpq = tile_rows // nq
    group = 8 // rpq
    groups = dates * bands // group
    steps = groups // 2
    all_dates = smoother.shape[0]
    dims = (nt, nq, slots, tile_rows, tile_cols, taps, grid_rows, grid_cols, group, rpq, steps, all_dates, bands)
    block = dates * bands * rpq
    smem = pl.BlockSpec(memory_space=pltpu.SMEM)
    vmem = pl.BlockSpec(memory_space=pltpu.VMEM)
    dma = pltpu.SemaphoreType.DMA
    out = pl.pallas_call(
        functools.partial(kernel, dims),
        out_shape=jax.ShapeDtypeStruct((all_dates, bands * rpq, tile_cols), jnp.float32),
        in_specs=[smem] * 5 + [vmem, vmem, pl.BlockSpec(memory_space=pl.ANY)],
        out_specs=vmem,
        scratch_shapes=[
            pltpu.VMEM((groups, group * grid_rows, grid_cols), jnp.bfloat16),
            pltpu.VMEM((slots, grid_cols, tile_cols), jnp.bfloat16),
            pltpu.VMEM((slots * tile_rows * group, group * grid_rows), jnp.bfloat16),
            pltpu.VMEM((slots, nq, block, grid_cols), jnp.bfloat16),
            pltpu.VMEM((slots, nq, block, grid_cols), jnp.bfloat16),
            pltpu.VMEM((slots, nq, block, tile_cols), jnp.float32),
            pltpu.VMEM((slots, nq, block, tile_cols), jnp.float32),
            pltpu.VMEM((nq, block, tile_cols), jnp.float32),
            dma((steps,)),
            dma((slots, nq)),
            dma((slots, nq)),
            dma((nq,)),
            dma((nq,)),
        ],
        compiler_params=pltpu.CompilerParams(
            collective_id=0, has_side_effects=True, vmem_limit_bytes=48 * 1024 * 1024),
        cost_estimate=pl.CostEstimate(flops=2_000_000_000, bytes_accessed=4_000_000, transcendentals=0),
    )(targets, row_offset, col_offset, mask.reshape(1, all_dates), smoother,
      jnp.transpose(coef_x[0], (0, 2, 1)), coef_y[0].reshape(slots * tile_rows, taps),
      granules.reshape(groups, group * grid_rows, grid_cols))
    return out.reshape(all_dates, bands, 1, rpq * tile_cols)


def solution(mesh):
    return jax.shard_map(
        body,
        mesh=mesh,
        in_specs=(
            P("date", None, "tile", None),
            P("tile", None, None, None),
            P("tile", None, None, None),
            P("tile", None),
            P("tile", None),
            P("tile", None),
            P(None, "tile"),
            P(),
        ),
        out_specs=P(None, None, "tile", "date"),
        check_vma=False,
    )
```

```python
import functools

import jax
import jax.numpy as jnp
from jax import lax
from jax.experimental import pallas as pl
from jax.experimental.pallas import tpu as pltpu
from jax.sharding import PartitionSpec as P

RADIUS = 2
MESH = pl.DeviceIdType.MESH
ROWS = 64


def kernel(dims, tgt_hbm, roff_hbm, coff_hbm, mask_hbm, smoother_hbm, cx_hbm, cy_hbm, g_hbm, out_ref,
           tgt, roff, coff, mask, smoother, cx_ref, cy_ref, small_sem, g, rx, ymat, high, low, part, recv, final,
           g_sem, send1, recv1, send2, recv2):
    nt, nq, slots, tile_rows, tile_cols, taps, grid_rows, grid_cols, group, rpq, steps, all_dates, bands = dims
    reaches = list(range(-RADIUS, RADIUS + 1))
    home = RADIUS
    others = [0, 4, 1, 3]
    tile = lax.axis_index("tile")
    date = lax.axis_index("date")

    def fetch(step):
        return pltpu.make_async_copy(g_hbm.at[pl.ds(2 * step, 2)], g.at[pl.ds(2 * step, 2)], g_sem.at[step])

    pairs = [(tgt_hbm, tgt), (roff_hbm, roff), (coff_hbm, coff), (cy_hbm, cy_ref), (cx_hbm, cx_ref),
             (mask_hbm, mask), (smoother_hbm, smoother)]
    small = [pltpu.make_async_copy(src, dst, small_sem.at[i]) for i, (src, dst) in enumerate(pairs)]
    for copy in small:
        copy.start()
    for step in range(steps):
        fetch(step).start()

    def inside(place):
        return jnp.logical_and(place >= 0, place < nt)

    barrier = pltpu.get_barrier_semaphore()
    for ri in others:
        there = tile + reaches[ri]

        @pl.when(inside(there))
        def _(there=there):
            pl.semaphore_signal(barrier, inc=1, device_id=(date, there), device_id_type=MESH)

    for c in range(1, nq):
        pl.semaphore_signal(barrier, inc=1, device_id=(lax.rem(date + c, nq), tile), device_id_type=MESH)

    for copy in small:
        copy.wait()

    m_count, c_count = slots * tile_rows * group, group * grid_rows
    per_slot = tile_rows * group
    m_e = lax.broadcasted_iota(jnp.int32, (m_count, slots * tile_rows), 0)
    n_e = lax.broadcasted_iota(jnp.int32, (m_count, slots * tile_rows), 1)

    def row_of(m):
        return ((m % per_slot) // (group * rpq)) * rpq + m % rpq

    aimed = jnp.full_like(n_e, -1)
    for k in range(slots):
        aimed = jnp.where(n_e // tile_rows == k, tgt[0, k], aimed)
    wanted = m_e // per_slot + (tile - RADIUS)
    pick = jnp.where(jnp.logical_and(row_of(m_e) == n_e % tile_rows, aimed == wanted), 1.0, 0.0)
    cy = jnp.dot(pick.astype(jnp.bfloat16), cy_ref[...], preferred_element_type=jnp.float32)
    m = lax.broadcasted_iota(jnp.int32, (m_count, c_count), 0)
    c = lax.broadcasted_iota(jnp.int32, (m_count, c_count), 1)
    shift = jnp.zeros_like(m)
    reach_tile = m // per_slot + (tile - RADIUS)
    for k in range(slots):
        shift = jnp.where(reach_tile == tgt[0, k], roff[0, k], shift)
    band_c = jnp.zeros_like(c)
    for b in range(1, group):
        band_c = jnp.where(c >= b * grid_rows, b, band_c)
    tap = c - band_c * grid_rows - 2 * row_of(m) - shift
    tap = jnp.where((m // rpq) % group == band_c, tap, -1)
    acc = jnp.zeros((m_count, c_count), jnp.float32)
    for t in range(taps):
        acc = jnp.where(tap == t, cy[:, t:t + 1], acc)
    ymat[...] = acc.astype(jnp.bfloat16)

    def build(r, carry):
        want = tile + (r - RADIUS)
        coef = jnp.zeros((taps, tile_cols), jnp.float32)
        off = jnp.int32(0)
        for k in range(slots):
            hit = tgt[0, k] == want
            coef = coef + cx_ref[k].astype(jnp.float32) * jnp.where(hit, 1.0, 0.0)
            off = off + jnp.where(hit, coff[0, k], 0)
        row = lax.broadcasted_iota(jnp.int32, (ROWS, tile_cols), 0)
        lane = lax.broadcasted_iota(jnp.int32, (ROWS, tile_cols), 1)
        base = row - 2 * lane - off
        for j in range(grid_cols // ROWS):
            tap = base + j * ROWS
            acc = jnp.zeros((ROWS, tile_cols), jnp.float32)
            for t in range(taps):
                acc = jnp.where(tap == t, coef[t:t + 1, :], acc)
            rx[r, j * ROWS:(j + 1) * ROWS, :] = acc.astype(jnp.bfloat16)
        return carry

    lax.fori_loop(0, slots, build, 0)

    for step in range(steps):
        fetch(step).wait()
        pair = [
            jnp.dot(ymat[...], g[2 * step + h], preferred_element_type=jnp.float32).reshape(slots * nq, 1, 8, grid_cols)
            for h in range(2)
        ]
        both = jnp.concatenate(pair, 1).reshape(slots, nq, 16, grid_cols)
        top = both.astype(jnp.bfloat16)
        high[:, :, step * 16:(step + 1) * 16, :] = top
        low[:, :, step * 16:(step + 1) * 16, :] = (both - top.astype(jnp.float32)).astype(jnp.bfloat16)

    peers = jnp.int32(nq - 1)
    for ri in others:
        peers = peers + jnp.where(inside(tile + reaches[ri]), 1, 0)
    pl.semaphore_wait(barrier, peers)

    def to_tile(ri, q):
        return pltpu.make_async_remote_copy(
            src_ref=part.at[ri, q], dst_ref=recv.at[ri, q], send_sem=send1.at[ri, q], recv_sem=recv1.at[ri, q],
            device_id=(date, tile + reaches[ri]), device_id_type=MESH)

    def to_date(q):
        return pltpu.make_async_remote_copy(
            src_ref=part.at[home, q], dst_ref=final.at[date], send_sem=send2.at[q], recv_sem=recv2.at[date],
            device_id=(q, tile), device_id_type=MESH)

    def from_date(q):
        return pltpu.make_async_remote_copy(
            src_ref=part.at[home, q], dst_ref=final.at[q], send_sem=send2.at[q], recv_sem=recv2.at[q],
            device_id=(q, tile), device_id_type=MESH)

    order = [nq // 2] + [s for s in range(1, nq) if s != nq // 2] + [0]
    blocks = [lax.rem(date + s, nq) for s in order]
    for q in blocks:
        for ri in others + [home]:
            part[ri, q] = (
                jnp.dot(high[ri, q], rx[ri], preferred_element_type=jnp.float32)
                + jnp.dot(low[ri, q], rx[ri], preferred_element_type=jnp.float32))
            if ri != home:

                @pl.when(inside(tile + reaches[ri]))
                def _(ri=ri, q=q):
                    to_tile(ri, q).start()

    for s, q in zip(order, blocks):
        for ri in others:

            @pl.when(inside(tile - reaches[ri]))
            def _(ri=ri, q=q):
                to_tile(ri, q).wait_recv()
                part[home, q] = part[home, q] + recv[ri, q]

        if s != 0:
            to_date(q).start()
        else:
            final[date] = part[home, q]

    for s, q in zip(order, blocks):
        if s != 0:
            from_date(q).wait_recv()

    rows = bands * rpq
    here = all_dates // nq
    valid = [mask[0, s].astype(jnp.float32) for s in range(all_dates)]

    def smooth(t, carry):
        total = jnp.zeros((rows, tile_cols), jnp.float32)
        weight = jnp.float32(0.0)
        for s in range(all_dates):
            w = smoother[t, s] * valid[s]
            weight = weight + w
            first = (s % here) * rows
            total = total + final[s // here, first:first + rows, :] * w
        out_ref[t] = total / jnp.full((rows, tile_cols), weight, jnp.float32)
        return carry

    lax.fori_loop(0, all_dates, smooth, 0)

    for s, q in zip(order, blocks):
        for ri in others:

            @pl.when(inside(tile + reaches[ri]))
            def _(ri=ri, q=q):
                to_tile(ri, q).wait_send()

        if s != 0:
            to_date(q).wait_send()


def body(granules, coef_x, coef_y, row_offset, col_offset, targets, mask, smoother):
    dates, bands, grid_rows, grid_cols = granules.shape
    _, slots, tile_cols, taps = coef_x.shape
    tile_rows = coef_y.shape[2]
    nq, nt = lax.axis_size("date"), lax.axis_size("tile")
    rpq = tile_rows // nq
    group = 8 // rpq
    groups = dates * bands // group
    steps = groups // 2
    all_dates = smoother.shape[0]
    dims = (nt, nq, slots, tile_rows, tile_cols, taps, grid_rows, grid_cols, group, rpq, steps, all_dates, bands)
    block = dates * bands * rpq
    vmem = pl.BlockSpec(memory_space=pltpu.VMEM)
    dma = pltpu.SemaphoreType.DMA
    out = pl.pallas_call(
        functools.partial(kernel, dims),
        out_shape=jax.ShapeDtypeStruct((all_dates, bands * rpq, tile_cols), jnp.float32),
        in_specs=[pl.BlockSpec(memory_space=pl.ANY)] * 8,
        out_specs=vmem,
        scratch_shapes=[
            pltpu.SMEM((1, slots), jnp.int32),
            pltpu.SMEM((1, slots), jnp.int32),
            pltpu.SMEM((1, slots), jnp.int32),
            pltpu.SMEM((1, all_dates), jnp.int32),
            pltpu.SMEM((all_dates, all_dates), jnp.float32),
            pltpu.VMEM((slots, taps, tile_cols), jnp.bfloat16),
            pltpu.VMEM((slots * tile_rows, taps), jnp.bfloat16),
            dma((7,)),
            pltpu.VMEM((groups, group * grid_rows, grid_cols), jnp.bfloat16),
            pltpu.VMEM((slots, grid_cols, tile_cols), jnp.bfloat16),
            pltpu.VMEM((slots * tile_rows * group, group * grid_rows), jnp.bfloat16),
            pltpu.VMEM((slots, nq, block, grid_cols), jnp.bfloat16),
            pltpu.VMEM((slots, nq, block, grid_cols), jnp.bfloat16),
            pltpu.VMEM((slots, nq, block, tile_cols), jnp.float32),
            pltpu.VMEM((slots, nq, block, tile_cols), jnp.float32),
            pltpu.VMEM((nq, block, tile_cols), jnp.float32),
            dma((steps,)),
            dma((slots, nq)),
            dma((slots, nq)),
            dma((nq,)),
            dma((nq,)),
        ],
        compiler_params=pltpu.CompilerParams(
            collective_id=0, has_side_effects=True, vmem_limit_bytes=60 * 1024 * 1024),
        cost_estimate=pl.CostEstimate(flops=2_000_000_000, bytes_accessed=4_000_000, transcendentals=0),
    )(targets, row_offset, col_offset, mask.reshape(1, all_dates), smoother,
      jnp.transpose(coef_x[0], (0, 2, 1)), coef_y[0].reshape(slots * tile_rows, taps),
      granules.reshape(groups, group * grid_rows, grid_cols))
    return out.reshape(all_dates, bands, 1, rpq * tile_cols)


def solution(mesh):
    return jax.shard_map(
        body,
        mesh=mesh,
        in_specs=(
            P("date", None, "tile", None),
            P("tile", None, None, None),
            P("tile", None, None, None),
            P("tile", None),
            P("tile", None),
            P("tile", None),
            P(None, "tile"),
            P(),
        ),
        out_specs=P(None, None, "tile", "date"),
        check_vma=False,
    )
```

```python
import functools

import jax
import jax.numpy as jnp
from jax import lax
from jax.experimental import pallas as pl
from jax.experimental.pallas import tpu as pltpu
from jax.sharding import PartitionSpec as P

MESH = pl.DeviceIdType.MESH
ROWS = 64


def kernel(dims, tgt_hbm, roff_hbm, coff_hbm, mask_hbm, smoother_hbm, cx_hbm, cy_hbm, g_hbm, out_ref, divisor_ref,
           tgt, roff, coff, mask, smoother, cx_ref, cy_ref, small_sem, g, rx, ymat, high, low, part, recv, final,
           g_sem, send1, recv1, send2, recv2):
    nt, nq, slots, tile_rows, tile_cols, taps, grid_rows, grid_cols, group, rpq, steps, all_dates, bands = dims
    diag, far, side, near, home = range(5)
    tile = lax.axis_index("tile")
    date = lax.axis_index("date")
    turn = 1 - 2 * (tile % 2)
    partner = tile + turn
    ahead = tile - 2 * turn
    behind = tile + 2 * turn
    has_ahead = jnp.logical_and(ahead >= 0, ahead < nt)
    has_behind = jnp.logical_and(behind >= 0, behind < nt)

    def tile_of(slot):
        aim = jnp.where(slot == diag, tile - turn, tile)
        aim = jnp.where(slot == far, ahead, aim)
        aim = jnp.where(slot == side, partner, aim)
        return jnp.where(slot == near, behind, aim)

    def fetch(step):
        return pltpu.make_async_copy(g_hbm.at[pl.ds(2 * step, 2)], g.at[pl.ds(2 * step, 2)], g_sem.at[step])

    pairs = [(tgt_hbm, tgt), (roff_hbm, roff), (coff_hbm, coff), (cy_hbm, cy_ref), (cx_hbm, cx_ref),
             (mask_hbm, mask), (smoother_hbm, smoother)]
    small = [pltpu.make_async_copy(src, dst, small_sem.at[i]) for i, (src, dst) in enumerate(pairs)]
    for copy in small:
        copy.start()
    for step in range(steps):
        fetch(step).start()

    barrier = pltpu.get_barrier_semaphore()
    pl.semaphore_signal(barrier, inc=1, device_id=(date, partner), device_id_type=MESH)
    for c in range(1, nq):
        pl.semaphore_signal(barrier, inc=1, device_id=(lax.rem(date + c, nq), tile), device_id_type=MESH)

    @pl.when(has_ahead)
    def _():
        pl.semaphore_signal(barrier, inc=1, device_id=(date, ahead), device_id_type=MESH)

    @pl.when(has_behind)
    def _():
        pl.semaphore_signal(barrier, inc=1, device_id=(date, behind), device_id_type=MESH)

    for copy in small:
        copy.wait()

    m_count, c_count = slots * tile_rows * group, group * grid_rows
    per_slot = tile_rows * group
    m_e = lax.broadcasted_iota(jnp.int32, (m_count, slots * tile_rows), 0)
    n_e = lax.broadcasted_iota(jnp.int32, (m_count, slots * tile_rows), 1)

    def row_of(m):
        return ((m % per_slot) // (group * rpq)) * rpq + m % rpq

    aimed = jnp.full_like(n_e, -1)
    for k in range(slots):
        aimed = jnp.where(n_e // tile_rows == k, tgt[0, k], aimed)
    pick = jnp.where(jnp.logical_and(row_of(m_e) == n_e % tile_rows, aimed == tile_of(m_e // per_slot)), 1.0, 0.0)
    cy = jnp.dot(pick.astype(jnp.bfloat16), cy_ref[...], preferred_element_type=jnp.float32)
    m = lax.broadcasted_iota(jnp.int32, (m_count, c_count), 0)
    c = lax.broadcasted_iota(jnp.int32, (m_count, c_count), 1)
    shift = jnp.zeros_like(m)
    reach_tile = tile_of(m // per_slot)
    for k in range(slots):
        shift = jnp.where(reach_tile == tgt[0, k], roff[0, k], shift)
    band_c = jnp.zeros_like(c)
    for b in range(1, group):
        band_c = jnp.where(c >= b * grid_rows, b, band_c)
    tap = c - band_c * grid_rows - 2 * row_of(m) - shift
    tap = jnp.where((m // rpq) % group == band_c, tap, -1)
    acc = jnp.zeros((m_count, c_count), jnp.float32)
    for t in range(taps):
        acc = jnp.where(tap == t, cy[:, t:t + 1], acc)
    ymat[...] = acc.astype(jnp.bfloat16)

    def build(r, carry):
        want = tile_of(r)
        coef = jnp.zeros((taps, tile_cols), jnp.float32)
        off = jnp.int32(0)
        for k in range(slots):
            hit = tgt[0, k] == want
            coef = coef + cx_ref[k].astype(jnp.float32) * jnp.where(hit, 1.0, 0.0)
            off = off + jnp.where(hit, coff[0, k], 0)
        row = lax.broadcasted_iota(jnp.int32, (ROWS, tile_cols), 0)
        lane = lax.broadcasted_iota(jnp.int32, (ROWS, tile_cols), 1)
        base = row - 2 * lane - off
        for j in range(grid_cols // ROWS):
            tap = base + j * ROWS
            acc = jnp.zeros((ROWS, tile_cols), jnp.float32)
            for t in range(taps):
                acc = jnp.where(tap == t, coef[t:t + 1, :], acc)
            rx[r, j * ROWS:(j + 1) * ROWS, :] = acc.astype(jnp.bfloat16)
        return carry

    def y_pass(first, count, step):
        rows = ymat[first * per_slot:(first + count) * per_slot, :]
        pair = [
            jnp.dot(rows, g[2 * step + h], preferred_element_type=jnp.float32).reshape(count * nq, 1, 8, grid_cols)
            for h in range(2)
        ]
        both = jnp.concatenate(pair, 1).reshape(count, nq, 16, grid_cols)
        top = both.astype(jnp.bfloat16)
        place = (slice(first, first + count), slice(None), slice(step * 16, (step + 1) * 16), slice(None))
        high[place] = top
        low[place] = (both - top.astype(jnp.float32)).astype(jnp.bfloat16)

    def x_pass(slot, q):
        part[slot, q] = (
            jnp.dot(high[slot, q], rx[slot], preferred_element_type=jnp.float32)
            + jnp.dot(low[slot, q], rx[slot], preferred_element_type=jnp.float32))

    order = [nq // 2] + [s for s in range(1, nq) if s != nq // 2] + [0]
    blocks = [lax.rem(date + s, nq) for s in order]

    def to_tile(slot, i):
        to = {diag: partner if i % 2 else ahead, far: ahead, side: partner, near: behind}[slot]
        q = blocks[i]
        return pltpu.make_async_remote_copy(
            src_ref=part.at[slot, q], dst_ref=recv.at[slot, q], send_sem=send1.at[slot, q], recv_sem=recv1.at[slot, q],
            device_id=(date, to), device_id_type=MESH)

    def to_date(q):
        return pltpu.make_async_remote_copy(
            src_ref=part.at[home, q], dst_ref=final.at[date], send_sem=send2.at[q], recv_sem=recv2.at[date],
            device_id=(q, tile), device_id_type=MESH)

    def from_date(q):
        return pltpu.make_async_remote_copy(
            src_ref=part.at[home, q], dst_ref=final.at[q], send_sem=send2.at[q], recv_sem=recv2.at[q],
            device_id=(q, tile), device_id_type=MESH)

    build(diag, 0)
    for step in range(steps):
        fetch(step).wait()
        y_pass(diag, 1, step)
    peers = nq + jnp.where(has_ahead, 1, 0) + jnp.where(has_behind, 1, 0)
    pl.semaphore_wait(barrier, peers)
    for i in range(nq):
        x_pass(diag, blocks[i])

        @pl.when(has_ahead)
        def _(i=i):
            to_tile(diag, i).start()

    lax.fori_loop(1, slots, build, 0)
    for step in range(steps):
        y_pass(far, slots - 1, step)

    for i in range(nq):
        q = blocks[i]
        x_pass(far, q)

        @pl.when(has_ahead)
        def _(i=i):
            to_tile(far, i).start()

        x_pass(side, q)
        if i % 2:
            to_tile(side, i).start()
        x_pass(near, q)
        if i % 2 == 0:

            @pl.when(has_behind)
            def _(i=i):
                to_tile(near, i).start()

        x_pass(home, q)
        joined = near if i % 2 else side

        @pl.when(has_behind)
        def _(i=i, q=q, joined=joined):
            to_tile(diag, i).wait_recv()
            part[joined, q] = part[joined, q] + recv[diag, q]
            if joined == near:
                to_tile(near, i).start()

        if joined == side:
            to_tile(side, i).start()

    def collect(i):
        q = blocks[i]
        to_tile(side, i).wait_recv()
        part[home, q] = part[home, q] + recv[side, q]

        @pl.when(has_behind)
        def _():
            to_tile(far, i).wait_recv()
            part[home, q] = part[home, q] + recv[far, q]

        @pl.when(has_ahead)
        def _():
            to_tile(near, i).wait_recv()
            part[home, q] = part[home, q] + recv[near, q]

    for i in range(nq - 1):
        collect(i)
        to_date(blocks[i]).start()
    for i in range(nq - 1):
        from_date(blocks[i]).wait_recv()

    rows = bands * rpq
    here = all_dates // nq

    def weight(t, s):
        return smoother[t, s] * mask[0, s].astype(jnp.float32)

    def smooth_others(t, carry):
        total = jnp.zeros((rows, tile_cols), jnp.float32)
        for i in range(nq - 1):
            q = blocks[i]
            for s in range(here):
                total = total + final[q, s * rows:(s + 1) * rows, :] * weight(t, q * here + s)
        out_ref[t] = total
        return carry

    lax.fori_loop(0, all_dates, smooth_others, 0)
    collect(nq - 1)

    def smooth_own(t, carry):
        total = out_ref[t]
        for s in range(here):
            total = total + part[home, date, s * rows:(s + 1) * rows, :] * weight(t, date * here + s)
        divisor = jnp.float32(0.0)
        for s in range(all_dates):
            divisor = divisor + weight(t, s)
        out_ref[t] = total
        divisor_ref[pl.ds(t, 1), :] = jnp.full((1, tile_cols), divisor, jnp.float32)
        return carry

    lax.fori_loop(0, all_dates, smooth_own, 0)

    for i in range(nq):
        to_tile(side, i).wait_send()

        @pl.when(has_ahead)
        def _(i=i):
            to_tile(diag, i).wait_send()
            to_tile(far, i).wait_send()

        @pl.when(has_behind)
        def _(i=i):
            to_tile(near, i).wait_send()

    for i in range(nq - 1):
        to_date(blocks[i]).wait_send()


def body(granules, coef_x, coef_y, row_offset, col_offset, targets, mask, smoother):
    dates, bands, grid_rows, grid_cols = granules.shape
    _, slots, tile_cols, taps = coef_x.shape
    tile_rows = coef_y.shape[2]
    nq, nt = lax.axis_size("date"), lax.axis_size("tile")
    rpq = tile_rows // nq
    group = 8 // rpq
    groups = dates * bands // group
    steps = groups // 2
    all_dates = smoother.shape[0]
    dims = (nt, nq, slots, tile_rows, tile_cols, taps, grid_rows, grid_cols, group, rpq, steps, all_dates, bands)
    block = dates * bands * rpq
    vmem = pl.BlockSpec(memory_space=pltpu.VMEM)
    dma = pltpu.SemaphoreType.DMA
    numerator, divisor = pl.pallas_call(
        functools.partial(kernel, dims),
        out_shape=(jax.ShapeDtypeStruct((all_dates, bands * rpq, tile_cols), jnp.float32),
                   jax.ShapeDtypeStruct((all_dates, tile_cols), jnp.float32)),
        in_specs=[pl.BlockSpec(memory_space=pl.ANY)] * 8,
        out_specs=(vmem, vmem),
        scratch_shapes=[
            pltpu.SMEM((1, slots), jnp.int32),
            pltpu.SMEM((1, slots), jnp.int32),
            pltpu.SMEM((1, slots), jnp.int32),
            pltpu.SMEM((1, all_dates), jnp.int32),
            pltpu.SMEM((all_dates, all_dates), jnp.float32),
            pltpu.VMEM((slots, taps, tile_cols), jnp.bfloat16),
            pltpu.VMEM((slots * tile_rows, taps), jnp.bfloat16),
            dma((7,)),
            pltpu.VMEM((groups, group * grid_rows, grid_cols), jnp.bfloat16),
            pltpu.VMEM((slots, grid_cols, tile_cols), jnp.bfloat16),
            pltpu.VMEM((slots * tile_rows * group, group * grid_rows), jnp.bfloat16),
            pltpu.VMEM((slots, nq, block, grid_cols), jnp.bfloat16),
            pltpu.VMEM((slots, nq, block, grid_cols), jnp.bfloat16),
            pltpu.VMEM((slots, nq, block, tile_cols), jnp.float32),
            pltpu.VMEM((slots, nq, block, tile_cols), jnp.float32),
            pltpu.VMEM((nq, block, tile_cols), jnp.float32),
            dma((steps,)),
            dma((slots, nq)),
            dma((slots, nq)),
            dma((nq,)),
            dma((nq,)),
        ],
        compiler_params=pltpu.CompilerParams(
            collective_id=0, has_side_effects=True, vmem_limit_bytes=60 * 1024 * 1024),
        cost_estimate=pl.CostEstimate(flops=2_000_000_000, bytes_accessed=4_000_000, transcendentals=0),
    )(targets, row_offset, col_offset, mask.reshape(1, all_dates), smoother,
      jnp.transpose(coef_x[0], (0, 2, 1)), coef_y[0].reshape(slots * tile_rows, taps),
      granules.reshape(groups, group * grid_rows, grid_cols))
    smoothed = numerator / divisor[:, None, :]
    return smoothed.reshape(all_dates, bands, 1, rpq * tile_cols)


def solution(mesh):
    return jax.shard_map(
        body,
        mesh=mesh,
        in_specs=(
            P("date", None, "tile", None),
            P("tile", None, None, None),
            P("tile", None, None, None),
            P("tile", None),
            P("tile", None),
            P("tile", None),
            P(None, "tile"),
            P(),
        ),
        out_specs=P(None, None, "tile", "date"),
        check_vma=False,
    )
```

```python
import functools

import jax
import jax.numpy as jnp
from jax import lax
from jax.experimental import pallas as pl
from jax.experimental.pallas import tpu as pltpu
from jax.sharding import PartitionSpec as P

MESH = pl.DeviceIdType.MESH
ROWS = 64


def kernel(dims, tgt_hbm, roff_hbm, coff_hbm, mask_hbm, smoother_hbm, cx_hbm, cy_hbm, g_hbm, out_ref, divisor_ref,
           tgt, roff, coff, mask, smoother, weights, cx_ref, cy_ref, small_sem, g, rx, ymat, parts, part, recv, final,
           g_sem, send1, recv1, send2, recv2):
    nt, nq, slots, tile_rows, tile_cols, taps, grid_rows, grid_cols, group, rpq, steps, all_dates, bands = dims
    diag, far, side, near, home = range(5)
    tile = lax.axis_index("tile")
    date = lax.axis_index("date")
    turn = 1 - 2 * (tile % 2)
    partner = tile + turn
    ahead = tile - 2 * turn
    behind = tile + 2 * turn
    has_ahead = jnp.logical_and(ahead >= 0, ahead < nt)
    has_behind = jnp.logical_and(behind >= 0, behind < nt)

    def tile_of(slot):
        aim = jnp.where(slot == diag, tile - turn, tile)
        aim = jnp.where(slot == far, ahead, aim)
        aim = jnp.where(slot == side, partner, aim)
        return jnp.where(slot == near, behind, aim)

    def fetch(step):
        return pltpu.make_async_copy(g_hbm.at[pl.ds(2 * step, 2)], g.at[pl.ds(2 * step, 2)], g_sem.at[step])

    pairs = [(tgt_hbm, tgt), (roff_hbm, roff), (coff_hbm, coff), (cy_hbm, cy_ref), (cx_hbm, cx_ref),
             (mask_hbm, mask), (smoother_hbm, smoother)]
    small = [pltpu.make_async_copy(src, dst, small_sem.at[i]) for i, (src, dst) in enumerate(pairs)]
    for copy in small:
        copy.start()
    for step in range(steps):
        fetch(step).start()

    barrier = pltpu.get_barrier_semaphore()
    pl.semaphore_signal(barrier, inc=1, device_id=(date, partner), device_id_type=MESH)
    for c in range(1, nq):
        pl.semaphore_signal(barrier, inc=1, device_id=(lax.rem(date + c, nq), tile), device_id_type=MESH)

    @pl.when(has_ahead)
    def _():
        pl.semaphore_signal(barrier, inc=1, device_id=(date, ahead), device_id_type=MESH)

    @pl.when(has_behind)
    def _():
        pl.semaphore_signal(barrier, inc=1, device_id=(date, behind), device_id_type=MESH)

    m_count, c_count = slots * tile_rows * group, group * grid_rows
    per_slot = tile_rows * group
    m_e = lax.broadcasted_iota(jnp.int32, (m_count, slots * tile_rows), 0)
    n_e = lax.broadcasted_iota(jnp.int32, (m_count, slots * tile_rows), 1)

    def row_of(m):
        return ((m % per_slot) // (group * rpq)) * rpq + m % rpq

    same_row = row_of(m_e) == n_e % tile_rows
    slot_e = n_e // tile_rows
    wanted_e = tile_of(m_e // per_slot)
    m = lax.broadcasted_iota(jnp.int32, (m_count, c_count), 0)
    c = lax.broadcasted_iota(jnp.int32, (m_count, c_count), 1)
    wanted = tile_of(m // per_slot)
    band_c = jnp.zeros_like(c)
    for b in range(1, group):
        band_c = jnp.where(c >= b * grid_rows, b, band_c)
    base = c - band_c * grid_rows - 2 * row_of(m)
    base = jnp.where((m // rpq) % group == band_c, base, -1)
    for copy in small:
        copy.wait()
    aimed = jnp.full_like(n_e, -1)
    for k in range(slots):
        aimed = jnp.where(slot_e == k, tgt[0, k], aimed)
    pick = jnp.where(jnp.logical_and(same_row, aimed == wanted_e), 1.0, 0.0)
    cy = jnp.dot(pick.astype(jnp.bfloat16), cy_ref[...], preferred_element_type=jnp.float32)
    shift = jnp.zeros_like(m)
    for k in range(slots):
        shift = jnp.where(wanted == tgt[0, k], roff[0, k], shift)
    tap = base - shift
    acc = jnp.zeros((m_count, c_count), jnp.float32)
    for t in range(taps):
        acc = jnp.where(tap == t, cy[:, t:t + 1], acc)
    ymat[...] = acc.astype(jnp.bfloat16)

    def build(r, carry):
        want = tile_of(r)
        coef = jnp.zeros((taps, tile_cols), jnp.float32)
        off = jnp.int32(0)
        for k in range(slots):
            hit = tgt[0, k] == want
            coef = coef + cx_ref[k].astype(jnp.float32) * jnp.where(hit, 1.0, 0.0)
            off = off + jnp.where(hit, coff[0, k], 0)
        row = lax.broadcasted_iota(jnp.int32, (ROWS, tile_cols), 0)
        lane = lax.broadcasted_iota(jnp.int32, (ROWS, tile_cols), 1)
        base = row - 2 * lane - off
        for j in range(grid_cols // ROWS):
            tap = base + j * ROWS
            acc = jnp.zeros((ROWS, tile_cols), jnp.float32)
            for t in range(taps):
                acc = jnp.where(tap == t, coef[t:t + 1, :], acc)
            rx[r, j * ROWS:(j + 1) * ROWS, :] = acc.astype(jnp.bfloat16)
        return carry

    def y_pass(first, count, step):
        rows = ymat[first * per_slot:(first + count) * per_slot, :]
        pair = [
            jnp.dot(rows, g[2 * step + h], preferred_element_type=jnp.float32).reshape(count * nq, 1, 8, grid_cols)
            for h in range(2)
        ]
        both = jnp.concatenate(pair, 1).reshape(count, nq, 16, grid_cols)
        top = both.astype(jnp.bfloat16)
        parts[first:first + count, :, 0, step * 16:(step + 1) * 16, :] = top
        parts[first:first + count, :, 1, step * 16:(step + 1) * 16, :] = (both - top.astype(jnp.float32)).astype(jnp.bfloat16)

    def x_pass(slot, q):
        block = part.shape[2]
        both = jnp.dot(parts[slot, q].reshape(2 * block, grid_cols), rx[slot], preferred_element_type=jnp.float32)
        part[slot, q] = both[:block] + both[block:]

    order = [nq // 2] + [s for s in range(1, nq) if s != nq // 2] + [0]
    blocks = [lax.rem(date + s, nq) for s in order]

    def to_tile(slot, i):
        to = {diag: partner if i % 2 else ahead, far: ahead, side: partner, near: behind}[slot]
        q = blocks[i]
        return pltpu.make_async_remote_copy(
            src_ref=part.at[slot, q], dst_ref=recv.at[slot, q], send_sem=send1.at[slot, q], recv_sem=recv1.at[slot, q],
            device_id=(date, to), device_id_type=MESH)

    def to_date(q):
        return pltpu.make_async_remote_copy(
            src_ref=part.at[home, q], dst_ref=final.at[date], send_sem=send2.at[q], recv_sem=recv2.at[date],
            device_id=(q, tile), device_id_type=MESH)

    def from_date(q):
        return pltpu.make_async_remote_copy(
            src_ref=part.at[home, q], dst_ref=final.at[q], send_sem=send2.at[q], recv_sem=recv2.at[q],
            device_id=(q, tile), device_id_type=MESH)

    build(diag, 0)
    for step in range(steps):
        fetch(step).wait()
        y_pass(diag, 1, step)
    peers = nq + jnp.where(has_ahead, 1, 0) + jnp.where(has_behind, 1, 0)
    pl.semaphore_wait(barrier, peers)
    for i in range(nq):
        x_pass(diag, blocks[i])

        @pl.when(has_ahead)
        def _(i=i):
            to_tile(diag, i).start()

    lax.fori_loop(1, slots, build, 0)
    for step in range(steps):
        y_pass(far, slots - 1, step)

    for i in range(nq):
        q = blocks[i]
        x_pass(far, q)

        @pl.when(has_ahead)
        def _(i=i):
            to_tile(far, i).start()

        x_pass(side, q)
        if i % 2:
            to_tile(side, i).start()
        x_pass(near, q)
        if i % 2 == 0:

            @pl.when(has_behind)
            def _(i=i):
                to_tile(near, i).start()

        x_pass(home, q)
        joined = near if i % 2 else side

        @pl.when(has_behind)
        def _(i=i, q=q, joined=joined):
            to_tile(diag, i).wait_recv()
            part[joined, q] = part[joined, q] + recv[diag, q]
            if joined == near:
                to_tile(near, i).start()

        if joined == side:
            to_tile(side, i).start()

    def collect(i):
        q = blocks[i]
        to_tile(side, i).wait_recv()
        part[home, q] = part[home, q] + recv[side, q]

        @pl.when(has_behind)
        def _():
            to_tile(far, i).wait_recv()
            part[home, q] = part[home, q] + recv[far, q]

        @pl.when(has_ahead)
        def _():
            to_tile(near, i).wait_recv()
            part[home, q] = part[home, q] + recv[near, q]

    def weigh(t, carry):
        divisor = jnp.float32(0.0)
        for s in range(all_dates):
            w = smoother[t, s] * mask[0, s].astype(jnp.float32)
            weights[t, s] = w
            divisor = divisor + w
        divisor_ref[pl.ds(t, 1), :] = jnp.full((1, tile_cols), divisor, jnp.float32)
        return carry

    lax.fori_loop(0, all_dates, weigh, 0)

    for i in range(nq - 1):
        collect(i)
        to_date(blocks[i]).start()

    rows = bands * rpq
    here = all_dates // nq

    def smooth(source, q, first):
        held = [source[s * rows:(s + 1) * rows, :] for s in range(here)]

        def one(t, carry):
            total = held[0] * weights[t, q * here]
            for s in range(1, here):
                total = total + held[s] * weights[t, q * here + s]
            out_ref[t] = total if first else out_ref[t] + total
            return carry

        lax.fori_loop(0, all_dates, one, 0, unroll=4)

    coming = sorted(order[:-1], key=lambda s: order.index(nq - s))
    for n, s in enumerate(coming[:-1]):
        q = lax.rem(date + s, nq)
        from_date(q).wait_recv()
        smooth(final.at[q], q, n == 0)
    collect(nq - 1)
    smooth(part.at[home, date], date, nq == 2)
    q = lax.rem(date + coming[-1], nq)
    from_date(q).wait_recv()
    smooth(final.at[q], q, False)

    for i in range(nq):
        to_tile(side, i).wait_send()

        @pl.when(has_ahead)
        def _(i=i):
            to_tile(diag, i).wait_send()
            to_tile(far, i).wait_send()

        @pl.when(has_behind)
        def _(i=i):
            to_tile(near, i).wait_send()

    for i in range(nq - 1):
        to_date(blocks[i]).wait_send()


def body(granules, coef_x, coef_y, row_offset, col_offset, targets, mask, smoother):
    dates, bands, grid_rows, grid_cols = granules.shape
    _, slots, tile_cols, taps = coef_x.shape
    tile_rows = coef_y.shape[2]
    nq, nt = lax.axis_size("date"), lax.axis_size("tile")
    rpq = tile_rows // nq
    group = 8 // rpq
    groups = dates * bands // group
    steps = groups // 2
    all_dates = smoother.shape[0]
    dims = (nt, nq, slots, tile_rows, tile_cols, taps, grid_rows, grid_cols, group, rpq, steps, all_dates, bands)
    block = dates * bands * rpq
    vmem = pl.BlockSpec(memory_space=pltpu.VMEM)
    dma = pltpu.SemaphoreType.DMA
    numerator, divisor = pl.pallas_call(
        functools.partial(kernel, dims),
        out_shape=(jax.ShapeDtypeStruct((all_dates, bands * rpq, tile_cols), jnp.float32),
                   jax.ShapeDtypeStruct((all_dates, tile_cols), jnp.float32)),
        in_specs=[pl.BlockSpec(memory_space=pl.ANY)] * 8,
        out_specs=(vmem, vmem),
        scratch_shapes=[
            pltpu.SMEM((1, slots), jnp.int32),
            pltpu.SMEM((1, slots), jnp.int32),
            pltpu.SMEM((1, slots), jnp.int32),
            pltpu.SMEM((1, all_dates), jnp.int32),
            pltpu.SMEM((all_dates, all_dates), jnp.float32),
            pltpu.SMEM((all_dates, all_dates), jnp.float32),
            pltpu.VMEM((slots, taps, tile_cols), jnp.bfloat16),
            pltpu.VMEM((slots * tile_rows, taps), jnp.bfloat16),
            dma((7,)),
            pltpu.VMEM((groups, group * grid_rows, grid_cols), jnp.bfloat16),
            pltpu.VMEM((slots, grid_cols, tile_cols), jnp.bfloat16),
            pltpu.VMEM((slots * tile_rows * group, group * grid_rows), jnp.bfloat16),
            pltpu.VMEM((slots, nq, 2, block, grid_cols), jnp.bfloat16),
            pltpu.VMEM((slots, nq, block, tile_cols), jnp.float32),
            pltpu.VMEM((slots, nq, block, tile_cols), jnp.float32),
            pltpu.VMEM((nq, block, tile_cols), jnp.float32),
            dma((steps,)),
            dma((slots, nq)),
            dma((slots, nq)),
            dma((nq,)),
            dma((nq,)),
        ],
        compiler_params=pltpu.CompilerParams(
            collective_id=0, has_side_effects=True, vmem_limit_bytes=60 * 1024 * 1024),
        cost_estimate=pl.CostEstimate(flops=2_000_000_000, bytes_accessed=4_000_000, transcendentals=0),
    )(targets, row_offset, col_offset, mask.reshape(1, all_dates), smoother,
      jnp.transpose(coef_x[0], (0, 2, 1)), coef_y[0].reshape(slots * tile_rows, taps),
      granules.reshape(groups, group * grid_rows, grid_cols))
    smoothed = numerator / divisor[:, None, :]
    return smoothed.reshape(all_dates, bands, 1, rpq * tile_cols)


def solution(mesh):
    return jax.shard_map(
        body,
        mesh=mesh,
        in_specs=(
            P("date", None, "tile", None),
            P("tile", None, None, None),
            P("tile", None, None, None),
            P("tile", None),
            P("tile", None),
            P("tile", None),
            P(None, "tile"),
            P(),
        ),
        out_specs=P(None, None, "tile", "date"),
        check_vma=False,
    )
```

```python
import functools

import jax
import jax.numpy as jnp
from jax import lax
from jax.experimental import pallas as pl
from jax.experimental.pallas import tpu as pltpu
from jax.sharding import PartitionSpec as P

MESH = pl.DeviceIdType.MESH
ROWS = 64


def kernel(dims, tgt_hbm, roff_hbm, coff_hbm, mask_hbm, smoother_hbm, cx_hbm, cy_hbm, g_hbm, out_ref, divisor_ref,
           tgt, roff, coff, mask, smoother, weights, cx_ref, cy_ref, small_sem, g, rx, ymat, parts, part, recv, final,
           g_sem, send1, recv1, send2, recv2):
    nt, nq, slots, tile_rows, tile_cols, taps, grid_rows, grid_cols, group, rpq, steps, all_dates, bands = dims
    diag, side, far, near, home = range(5)
    tile = lax.axis_index("tile")
    date = lax.axis_index("date")
    turn = 1 - 2 * (tile % 2)
    partner = tile + turn
    ahead = tile - 2 * turn
    behind = tile + 2 * turn
    has_ahead = jnp.logical_and(ahead >= 0, ahead < nt)
    has_behind = jnp.logical_and(behind >= 0, behind < nt)

    def tile_of(slot):
        aim = jnp.where(slot == diag, tile - turn, tile)
        aim = jnp.where(slot == far, ahead, aim)
        aim = jnp.where(slot == side, partner, aim)
        return jnp.where(slot == near, behind, aim)

    def fetch(step):
        return pltpu.make_async_copy(g_hbm.at[pl.ds(2 * step, 2)], g.at[pl.ds(2 * step, 2)], g_sem.at[step])

    pairs = [(tgt_hbm, tgt), (roff_hbm, roff), (coff_hbm, coff), (cy_hbm, cy_ref), (cx_hbm, cx_ref),
             (mask_hbm, mask), (smoother_hbm, smoother)]
    small = [pltpu.make_async_copy(src, dst, small_sem.at[i]) for i, (src, dst) in enumerate(pairs)]
    for copy in small:
        copy.start()
    for step in range(steps):
        fetch(step).start()

    barrier = pltpu.get_barrier_semaphore()
    pl.semaphore_signal(barrier, inc=1, device_id=(date, partner), device_id_type=MESH)
    for c in range(1, nq):
        pl.semaphore_signal(barrier, inc=1, device_id=(lax.rem(date + c, nq), tile), device_id_type=MESH)

    @pl.when(has_ahead)
    def _():
        pl.semaphore_signal(barrier, inc=1, device_id=(date, ahead), device_id_type=MESH)

    @pl.when(has_behind)
    def _():
        pl.semaphore_signal(barrier, inc=1, device_id=(date, behind), device_id_type=MESH)

    m_count, c_count = slots * tile_rows * group, group * grid_rows
    per_slot = tile_rows * group
    m_e = lax.broadcasted_iota(jnp.int32, (m_count, slots * tile_rows), 0)
    n_e = lax.broadcasted_iota(jnp.int32, (m_count, slots * tile_rows), 1)

    def row_of(m):
        return ((m % per_slot) // (group * rpq)) * rpq + m % rpq

    same_row = row_of(m_e) == n_e % tile_rows
    slot_e = n_e // tile_rows
    wanted_e = tile_of(m_e // per_slot)
    m = lax.broadcasted_iota(jnp.int32, (m_count, c_count), 0)
    c = lax.broadcasted_iota(jnp.int32, (m_count, c_count), 1)
    wanted = tile_of(m // per_slot)
    band_c = jnp.zeros_like(c)
    for b in range(1, group):
        band_c = jnp.where(c >= b * grid_rows, b, band_c)
    base = c - band_c * grid_rows - 2 * row_of(m)
    base = jnp.where((m // rpq) % group == band_c, base, -1)
    for copy in small:
        copy.wait()
    aimed = jnp.full_like(n_e, -1)
    for k in range(slots):
        aimed = jnp.where(slot_e == k, tgt[0, k], aimed)
    pick = jnp.where(jnp.logical_and(same_row, aimed == wanted_e), 1.0, 0.0)
    cy = jnp.dot(pick.astype(jnp.bfloat16), cy_ref[...], preferred_element_type=jnp.float32)
    shift = jnp.zeros_like(m)
    for k in range(slots):
        shift = jnp.where(wanted == tgt[0, k], roff[0, k], shift)
    tap = base - shift
    acc = jnp.zeros((m_count, c_count), jnp.float32)
    for t in range(taps):
        acc = jnp.where(tap == t, cy[:, t:t + 1], acc)
    ymat[...] = acc.astype(jnp.bfloat16)

    def build(r, carry):
        want = tile_of(r)
        coef = jnp.zeros((taps, tile_cols), jnp.float32)
        off = jnp.int32(0)
        for k in range(slots):
            hit = tgt[0, k] == want
            coef = coef + cx_ref[k].astype(jnp.float32) * jnp.where(hit, 1.0, 0.0)
            off = off + jnp.where(hit, coff[0, k], 0)
        row = lax.broadcasted_iota(jnp.int32, (ROWS, tile_cols), 0)
        lane = lax.broadcasted_iota(jnp.int32, (ROWS, tile_cols), 1)
        base = row - 2 * lane - off
        for j in range(grid_cols // ROWS):
            tap = base + j * ROWS
            acc = jnp.zeros((ROWS, tile_cols), jnp.float32)
            for t in range(taps):
                acc = jnp.where(tap == t, coef[t:t + 1, :], acc)
            rx[r, j * ROWS:(j + 1) * ROWS, :] = acc.astype(jnp.bfloat16)
        return carry

    def y_pass(first, count, step):
        rows = ymat[first * per_slot:(first + count) * per_slot, :]
        pair = [
            jnp.dot(rows, g[2 * step + h], preferred_element_type=jnp.float32).reshape(count * nq, 1, 8, grid_cols)
            for h in range(2)
        ]
        both = jnp.concatenate(pair, 1).reshape(count, nq, 16, grid_cols)
        top = both.astype(jnp.bfloat16)
        parts[first:first + count, :, 0, step * 16:(step + 1) * 16, :] = top
        parts[first:first + count, :, 1, step * 16:(step + 1) * 16, :] = (both - top.astype(jnp.float32)).astype(jnp.bfloat16)

    def x_pass(slot, q):
        block = part.shape[2]
        both = jnp.dot(parts[slot, q].reshape(2 * block, grid_cols), rx[slot], preferred_element_type=jnp.float32)
        part[slot, q] = both[:block] + both[block:]

    order = [nq // 2] + [s for s in range(1, nq) if s != nq // 2] + [0]
    blocks = [lax.rem(date + s, nq) for s in order]

    def to_tile(slot, i):
        to = {diag: partner if i % 2 else ahead, far: ahead, side: partner, near: behind}[slot]
        q = blocks[i]
        return pltpu.make_async_remote_copy(
            src_ref=part.at[slot, q], dst_ref=recv.at[slot, q], send_sem=send1.at[slot, q], recv_sem=recv1.at[slot, q],
            device_id=(date, to), device_id_type=MESH)

    def to_date(q):
        return pltpu.make_async_remote_copy(
            src_ref=part.at[home, q], dst_ref=final.at[date], send_sem=send2.at[q], recv_sem=recv2.at[date],
            device_id=(q, tile), device_id_type=MESH)

    def from_date(q):
        return pltpu.make_async_remote_copy(
            src_ref=part.at[home, q], dst_ref=final.at[q], send_sem=send2.at[q], recv_sem=recv2.at[q],
            device_id=(q, tile), device_id_type=MESH)

    build(diag, 0)
    build(side, 0)
    for step in range(steps):
        fetch(step).wait()
    for step in range(steps):
        y_pass(diag, 2, step)
    peers = nq + jnp.where(has_ahead, 1, 0) + jnp.where(has_behind, 1, 0)
    pl.semaphore_wait(barrier, peers)
    for i in range(nq):
        x_pass(diag, blocks[i])

    @pl.when(has_ahead)
    def _():
        for i in range(nq):
            to_tile(diag, i).start()

    for i in range(nq):
        x_pass(side, blocks[i])
    for i in range(1, nq, 2):
        to_tile(side, i).start()

    for r in (far, near, home):
        build(r, 0)
    for step in range(steps):
        y_pass(far, 3, step)

    def relay(i):
        joined = near if i % 2 else side
        q = blocks[i]

        @pl.when(has_behind)
        def _():
            to_tile(diag, i).wait_recv()
            part[joined, q] = part[joined, q] + recv[diag, q]
            if joined == near:
                to_tile(near, i).start()

        if joined == side:
            to_tile(side, i).start()

    relay(0)
    for i in range(nq):
        q = blocks[i]
        for slot in (far, near, home):
            x_pass(slot, q)

        @pl.when(has_ahead)
        def _(i=i):
            to_tile(far, i).start()

        if i % 2 == 0:

            @pl.when(has_behind)
            def _(i=i):
                to_tile(near, i).start()

        if i > 0:
            relay(i)

    def collect(i):
        q = blocks[i]
        to_tile(side, i).wait_recv()
        part[home, q] = part[home, q] + recv[side, q]

        @pl.when(has_behind)
        def _():
            to_tile(far, i).wait_recv()
            part[home, q] = part[home, q] + recv[far, q]

        @pl.when(has_ahead)
        def _():
            to_tile(near, i).wait_recv()
            part[home, q] = part[home, q] + recv[near, q]

    def weigh(t, carry):
        divisor = jnp.float32(0.0)
        for s in range(all_dates):
            w = smoother[t, s] * mask[0, s].astype(jnp.float32)
            weights[t, s] = w
            divisor = divisor + w
        divisor_ref[pl.ds(t, 1), :] = jnp.full((1, tile_cols), divisor, jnp.float32)
        return carry

    lax.fori_loop(0, all_dates, weigh, 0)

    for i in range(nq - 1):
        collect(i)
        to_date(blocks[i]).start()

    rows = bands * rpq
    here = all_dates // nq

    def smooth(source, q, first):
        held = [source[s * rows:(s + 1) * rows, :] for s in range(here)]

        def one(t, carry):
            total = held[0] * weights[t, q * here]
            for s in range(1, here):
                total = total + held[s] * weights[t, q * here + s]
            out_ref[t] = total if first else out_ref[t] + total
            return carry

        lax.fori_loop(0, all_dates, one, 0, unroll=4)

    coming = sorted(order[:-1], key=lambda s: order.index(nq - s))
    for n, s in enumerate(coming[:-1]):
        q = lax.rem(date + s, nq)
        from_date(q).wait_recv()
        smooth(final.at[q], q, n == 0)
    collect(nq - 1)
    smooth(part.at[home, date], date, nq == 2)
    q = lax.rem(date + coming[-1], nq)
    from_date(q).wait_recv()
    smooth(final.at[q], q, False)

    for i in range(nq):
        to_tile(side, i).wait_send()

        @pl.when(has_ahead)
        def _(i=i):
            to_tile(diag, i).wait_send()
            to_tile(far, i).wait_send()

        @pl.when(has_behind)
        def _(i=i):
            to_tile(near, i).wait_send()

    for i in range(nq - 1):
        to_date(blocks[i]).wait_send()


def body(granules, coef_x, coef_y, row_offset, col_offset, targets, mask, smoother):
    dates, bands, grid_rows, grid_cols = granules.shape
    _, slots, tile_cols, taps = coef_x.shape
    tile_rows = coef_y.shape[2]
    nq, nt = lax.axis_size("date"), lax.axis_size("tile")
    rpq = tile_rows // nq
    group = 8 // rpq
    groups = dates * bands // group
    steps = groups // 2
    all_dates = smoother.shape[0]
    dims = (nt, nq, slots, tile_rows, tile_cols, taps, grid_rows, grid_cols, group, rpq, steps, all_dates, bands)
    block = dates * bands * rpq
    vmem = pl.BlockSpec(memory_space=pltpu.VMEM)
    dma = pltpu.SemaphoreType.DMA
    numerator, divisor = pl.pallas_call(
        functools.partial(kernel, dims),
        out_shape=(jax.ShapeDtypeStruct((all_dates, bands * rpq, tile_cols), jnp.float32),
                   jax.ShapeDtypeStruct((all_dates, tile_cols), jnp.float32)),
        in_specs=[pl.BlockSpec(memory_space=pl.ANY)] * 8,
        out_specs=(vmem, vmem),
        scratch_shapes=[
            pltpu.SMEM((1, slots), jnp.int32),
            pltpu.SMEM((1, slots), jnp.int32),
            pltpu.SMEM((1, slots), jnp.int32),
            pltpu.SMEM((1, all_dates), jnp.int32),
            pltpu.SMEM((all_dates, all_dates), jnp.float32),
            pltpu.SMEM((all_dates, all_dates), jnp.float32),
            pltpu.VMEM((slots, taps, tile_cols), jnp.bfloat16),
            pltpu.VMEM((slots * tile_rows, taps), jnp.bfloat16),
            dma((7,)),
            pltpu.VMEM((groups, group * grid_rows, grid_cols), jnp.bfloat16),
            pltpu.VMEM((slots, grid_cols, tile_cols), jnp.bfloat16),
            pltpu.VMEM((slots * tile_rows * group, group * grid_rows), jnp.bfloat16),
            pltpu.VMEM((slots, nq, 2, block, grid_cols), jnp.bfloat16),
            pltpu.VMEM((slots, nq, block, tile_cols), jnp.float32),
            pltpu.VMEM((slots, nq, block, tile_cols), jnp.float32),
            pltpu.VMEM((nq, block, tile_cols), jnp.float32),
            dma((steps,)),
            dma((slots, nq)),
            dma((slots, nq)),
            dma((nq,)),
            dma((nq,)),
        ],
        compiler_params=pltpu.CompilerParams(
            collective_id=0, has_side_effects=True, vmem_limit_bytes=60 * 1024 * 1024),
        cost_estimate=pl.CostEstimate(flops=2_000_000_000, bytes_accessed=4_000_000, transcendentals=0),
    )(targets, row_offset, col_offset, mask.reshape(1, all_dates), smoother,
      jnp.transpose(coef_x[0], (0, 2, 1)), coef_y[0].reshape(slots * tile_rows, taps),
      granules.reshape(groups, group * grid_rows, grid_cols))
    smoothed = numerator / divisor[:, None, :]
    return smoothed.reshape(all_dates, bands, 1, rpq * tile_cols)


def solution(mesh):
    return jax.shard_map(
        body,
        mesh=mesh,
        in_specs=(
            P("date", None, "tile", None),
            P("tile", None, None, None),
            P("tile", None, None, None),
            P("tile", None),
            P("tile", None),
            P("tile", None),
            P(None, "tile"),
            P(),
        ),
        out_specs=P(None, None, "tile", "date"),
        check_vma=False,
    )
```

```python
import functools

import jax
import jax.numpy as jnp
from jax import lax
from jax.experimental import pallas as pl
from jax.experimental.pallas import tpu as pltpu
from jax.sharding import PartitionSpec as P

MESH = pl.DeviceIdType.MESH
ROWS = 64


def log(size):
    assert size & (size - 1) == 0
    return size.bit_length() - 1


def kernel(dims, tgt_hbm, roff_hbm, coff_hbm, mask_hbm, smoother_hbm, cx_hbm, cy_hbm, g_hbm, out_ref, divisor_ref,
           tgt, roff, coff, mask, smoother, weights, cx_ref, cy_ref, small_sem, g, rx, ymat, parts, part, recv, final,
           g_sem, send1, recv1, send2, recv2):
    nt, nq, slots, tile_rows, tile_cols, taps, grid_rows, grid_cols, group, rpq, steps, all_dates, bands = dims
    diag, side, far, near, home = range(5)
    tile = lax.axis_index("tile")
    date = lax.axis_index("date")
    turn = 1 - 2 * (tile % 2)
    partner = tile + turn
    ahead = tile - 2 * turn
    behind = tile + 2 * turn
    has_ahead = jnp.logical_and(ahead >= 0, ahead < nt)
    has_behind = jnp.logical_and(behind >= 0, behind < nt)

    def tile_of(slot):
        aim = jnp.where(slot == diag, tile - turn, tile)
        aim = jnp.where(slot == far, ahead, aim)
        aim = jnp.where(slot == side, partner, aim)
        return jnp.where(slot == near, behind, aim)

    def fetch(step):
        return pltpu.make_async_copy(g_hbm.at[pl.ds(2 * step, 2)], g.at[pl.ds(2 * step, 2)], g_sem.at[step])

    pairs = [(tgt_hbm, tgt), (roff_hbm, roff), (coff_hbm, coff), (cy_hbm, cy_ref), (cx_hbm, cx_ref),
             (mask_hbm, mask), (smoother_hbm, smoother)]
    small = [pltpu.make_async_copy(src, dst, small_sem.at[i]) for i, (src, dst) in enumerate(pairs)]
    for copy in small:
        copy.start()
    for step in range(steps):
        fetch(step).start()

    barrier = pltpu.get_barrier_semaphore()
    pl.semaphore_signal(barrier, inc=1, device_id=(date, partner), device_id_type=MESH)
    for c in range(1, nq):
        pl.semaphore_signal(barrier, inc=1, device_id=(lax.rem(date + c, nq), tile), device_id_type=MESH)

    @pl.when(has_ahead)
    def _():
        pl.semaphore_signal(barrier, inc=1, device_id=(date, ahead), device_id_type=MESH)

    @pl.when(has_behind)
    def _():
        pl.semaphore_signal(barrier, inc=1, device_id=(date, behind), device_id_type=MESH)

    m_count, c_count = slots * tile_rows * group, group * grid_rows
    per_slot = tile_rows * group
    m_e = lax.broadcasted_iota(jnp.int32, (m_count, slots * tile_rows), 0)
    n_e = lax.broadcasted_iota(jnp.int32, (m_count, slots * tile_rows), 1)

    def row_of(m):
        return ((m & (per_slot - 1)) >> log(group * rpq)) * rpq + (m & (rpq - 1))

    same_row = row_of(m_e) == (n_e & (tile_rows - 1))
    slot_e = n_e >> log(tile_rows)
    wanted_e = tile_of(m_e >> log(per_slot))
    m = lax.broadcasted_iota(jnp.int32, (m_count, c_count), 0)
    c = lax.broadcasted_iota(jnp.int32, (m_count, c_count), 1)
    wanted = tile_of(m >> log(per_slot))
    band_c = jnp.zeros_like(c)
    for b in range(1, group):
        band_c = jnp.where(c >= b * grid_rows, b, band_c)
    base = c - band_c * grid_rows - 2 * row_of(m)
    base = jnp.where(((m >> log(rpq)) & (group - 1)) == band_c, base, -1)
    for copy in small:
        copy.wait()
    aimed = jnp.full_like(n_e, -1)
    for k in range(slots):
        aimed = jnp.where(slot_e == k, tgt[0, k], aimed)
    pick = jnp.where(jnp.logical_and(same_row, aimed == wanted_e), 1.0, 0.0)
    cy = jnp.dot(pick.astype(jnp.bfloat16), cy_ref[...], preferred_element_type=jnp.float32)
    shift = jnp.zeros_like(m)
    for k in range(slots):
        shift = jnp.where(wanted == tgt[0, k], roff[0, k], shift)
    tap = base - shift
    acc = jnp.zeros((m_count, c_count), jnp.float32)
    for t in range(taps):
        acc = jnp.where(tap == t, cy[:, t:t + 1], acc)
    ymat[...] = acc.astype(jnp.bfloat16)

    def build(r, carry):
        want = tile_of(r)
        coef = jnp.zeros((taps, tile_cols), jnp.float32)
        off = jnp.int32(0)
        for k in range(slots):
            hit = tgt[0, k] == want
            coef = coef + cx_ref[k].astype(jnp.float32) * jnp.where(hit, 1.0, 0.0)
            off = off + jnp.where(hit, coff[0, k], 0)
        row = lax.broadcasted_iota(jnp.int32, (ROWS, tile_cols), 0)
        lane = lax.broadcasted_iota(jnp.int32, (ROWS, tile_cols), 1)
        base = row - 2 * lane - off
        for j in range(grid_cols // ROWS):
            tap = base + j * ROWS
            acc = jnp.zeros((ROWS, tile_cols), jnp.float32)
            for t in range(taps):
                acc = jnp.where(tap == t, coef[t:t + 1, :], acc)
            rx[r, j * ROWS:(j + 1) * ROWS, :] = acc.astype(jnp.bfloat16)
        return carry

    def y_pass(first, count, step):
        rows = ymat[first * per_slot:(first + count) * per_slot, :]
        pair = [
            jnp.dot(rows, g[2 * step + h], preferred_element_type=jnp.float32).reshape(count * nq, 1, 8, grid_cols)
            for h in range(2)
        ]
        both = jnp.concatenate(pair, 1).reshape(count, nq, 16, grid_cols)
        top = both.astype(jnp.bfloat16)
        place = pl.ds(pl.multiple_of(step * 16, 16), 16)
        parts[first:first + count, :, 0, place, :] = top
        parts[first:first + count, :, 1, place, :] = (both - top.astype(jnp.float32)).astype(jnp.bfloat16)

    def x_pass(slot, q):
        block = part.shape[2]
        both = jnp.dot(parts[slot, q].reshape(2 * block, grid_cols), rx[slot], preferred_element_type=jnp.float32)
        part[slot, q] = both[:block] + both[block:]

    order = list(range(1, nq)) + [0]

    def block_at(i):
        return lax.rem(date + 1 + i, nq)

    def to_tile(slot, i):
        q = block_at(i)
        to = jnp.where(slot == near, behind, jnp.where(slot == side, partner, ahead))
        to = jnp.where(jnp.logical_and(slot == diag, i % 2 == 1), partner, to)
        return pltpu.make_async_remote_copy(
            src_ref=part.at[slot, q], dst_ref=recv.at[slot, q], send_sem=send1.at[slot, q], recv_sem=recv1.at[slot, q],
            device_id=(date, to), device_id_type=MESH)

    def to_date(q):
        return pltpu.make_async_remote_copy(
            src_ref=part.at[home, q], dst_ref=final.at[date], send_sem=send2.at[q], recv_sem=recv2.at[date],
            device_id=(q, tile), device_id_type=MESH)

    def from_date(q):
        return pltpu.make_async_remote_copy(
            src_ref=part.at[home, q], dst_ref=final.at[q], send_sem=send2.at[q], recv_sem=recv2.at[q],
            device_id=(q, tile), device_id_type=MESH)

    def y_loop(first, count):
        def one(step, carry):
            y_pass(first, count, step)
            return carry

        lax.fori_loop(0, steps, one, 0, unroll=2 if steps % 2 == 0 else 1)

    lax.fori_loop(diag, side + 1, build, 0)
    for step in range(steps):
        fetch(step).wait()
    y_loop(diag, 2)
    peers = nq + jnp.where(has_ahead, 1, 0) + jnp.where(has_behind, 1, 0)
    pl.semaphore_wait(barrier, peers)

    def phase1(i, carry):
        q = block_at(i)
        for slot in (diag, side):
            x_pass(slot, q)

        @pl.when(has_ahead)
        def _():
            to_tile(diag, i).start()

        @pl.when(i % 2 == 1)
        def _():
            to_tile(side, i).start()

        return carry

    lax.fori_loop(0, nq, phase1, 0)

    lax.fori_loop(far, home + 1, build, 0)
    y_loop(far, 3)

    def phase2(i, carry):
        q = block_at(i)
        for slot in (far, near, home):
            x_pass(slot, q)

        @pl.when(has_ahead)
        def _():
            to_tile(far, i).start()

        @pl.when(jnp.logical_and(has_behind, i % 2 == 0))
        def _():
            to_tile(near, i).start()

        joined = jnp.where(i % 2 == 1, near, side)

        @pl.when(has_behind)
        def _():
            to_tile(diag, i).wait_recv()
            part[joined, q] = part[joined, q] + recv[diag, q]

        @pl.when(jnp.logical_or(has_behind, i % 2 == 0))
        def _():
            to_tile(joined, i).start()

        return carry

    lax.fori_loop(0, nq, phase2, 0)

    def collect(i):
        q = block_at(i)
        to_tile(side, i).wait_recv()
        part[home, q] = part[home, q] + recv[side, q]

        @pl.when(has_behind)
        def _():
            to_tile(far, i).wait_recv()
            part[home, q] = part[home, q] + recv[far, q]

        @pl.when(has_ahead)
        def _():
            to_tile(near, i).wait_recv()
            part[home, q] = part[home, q] + recv[near, q]

    def weigh(t, carry):
        divisor = jnp.float32(0.0)
        for s in range(all_dates):
            w = smoother[t, s] * mask[0, s].astype(jnp.float32)
            weights[t, s] = w
            divisor = divisor + w
        divisor_ref[pl.ds(t, 1), :] = jnp.full((1, tile_cols), divisor, jnp.float32)
        return carry

    lax.fori_loop(0, all_dates, weigh, 0)

    def gather(i, carry):
        collect(i)
        to_date(block_at(i)).start()
        return carry

    lax.fori_loop(0, nq - 1, gather, 0)

    rows = bands * rpq
    here = all_dates // nq

    def smooth(source, q, first):
        held = [source[s * rows:(s + 1) * rows, :] for s in range(here)]

        def one(t, carry):
            total = held[0] * weights[t, q * here]
            for s in range(1, here):
                total = total + held[s] * weights[t, q * here + s]
            out_ref[t] = total if first else out_ref[t] + total
            return carry

        lax.fori_loop(0, all_dates, one, 0, unroll=2)

    coming = sorted(order[:-1], key=lambda s: order.index(nq - s))
    for n, s in enumerate(coming[:-1]):
        q = lax.rem(date + s, nq)
        from_date(q).wait_recv()
        smooth(final.at[q], q, n == 0)
    collect(nq - 1)
    smooth(part.at[home, date], date, nq == 2)
    q = lax.rem(date + coming[-1], nq)
    from_date(q).wait_recv()
    smooth(final.at[q], q, False)

    def drain(i, carry):
        to_tile(side, i).wait_send()

        @pl.when(has_ahead)
        def _():
            to_tile(diag, i).wait_send()
            to_tile(far, i).wait_send()

        @pl.when(has_behind)
        def _():
            to_tile(near, i).wait_send()

        return carry

    lax.fori_loop(0, nq, drain, 0)
    for i in range(nq - 1):
        to_date(block_at(i)).wait_send()


def body(granules, coef_x, coef_y, row_offset, col_offset, targets, mask, smoother):
    dates, bands, grid_rows, grid_cols = granules.shape
    _, slots, tile_cols, taps = coef_x.shape
    tile_rows = coef_y.shape[2]
    nq, nt = lax.axis_size("date"), lax.axis_size("tile")
    rpq = tile_rows // nq
    group = 8 // rpq
    groups = dates * bands // group
    steps = groups // 2
    all_dates = smoother.shape[0]
    dims = (nt, nq, slots, tile_rows, tile_cols, taps, grid_rows, grid_cols, group, rpq, steps, all_dates, bands)
    block = dates * bands * rpq
    vmem = pl.BlockSpec(memory_space=pltpu.VMEM)
    dma = pltpu.SemaphoreType.DMA
    numerator, divisor = pl.pallas_call(
        functools.partial(kernel, dims),
        out_shape=(jax.ShapeDtypeStruct((all_dates, bands * rpq, tile_cols), jnp.float32),
                   jax.ShapeDtypeStruct((all_dates, tile_cols), jnp.float32)),
        in_specs=[pl.BlockSpec(memory_space=pl.ANY)] * 8,
        out_specs=(vmem, vmem),
        scratch_shapes=[
            pltpu.SMEM((1, slots), jnp.int32),
            pltpu.SMEM((1, slots), jnp.int32),
            pltpu.SMEM((1, slots), jnp.int32),
            pltpu.SMEM((1, all_dates), jnp.int32),
            pltpu.SMEM((all_dates, all_dates), jnp.float32),
            pltpu.SMEM((all_dates, all_dates), jnp.float32),
            pltpu.VMEM((slots, taps, tile_cols), jnp.bfloat16),
            pltpu.VMEM((slots * tile_rows, taps), jnp.bfloat16),
            dma((7,)),
            pltpu.VMEM((groups, group * grid_rows, grid_cols), jnp.bfloat16),
            pltpu.VMEM((slots, grid_cols, tile_cols), jnp.bfloat16),
            pltpu.VMEM((slots * tile_rows * group, group * grid_rows), jnp.bfloat16),
            pltpu.VMEM((slots, nq, 2, block, grid_cols), jnp.bfloat16),
            pltpu.VMEM((slots, nq, block, tile_cols), jnp.float32),
            pltpu.VMEM((slots, nq, block, tile_cols), jnp.float32),
            pltpu.VMEM((nq, block, tile_cols), jnp.float32),
            dma((steps,)),
            dma((slots, nq)),
            dma((slots, nq)),
            dma((nq,)),
            dma((nq,)),
        ],
        compiler_params=pltpu.CompilerParams(
            collective_id=0, has_side_effects=True, vmem_limit_bytes=60 * 1024 * 1024),
        cost_estimate=pl.CostEstimate(flops=2_000_000_000, bytes_accessed=4_000_000, transcendentals=0),
    )(targets, row_offset, col_offset, mask.reshape(1, all_dates), smoother,
      jnp.transpose(coef_x[0], (0, 2, 1)), coef_y[0].reshape(slots * tile_rows, taps),
      granules.reshape(groups, group * grid_rows, grid_cols))
    smoothed = numerator / divisor[:, None, :]
    return smoothed.reshape(all_dates, bands, 1, rpq * tile_cols)


def solution(mesh):
    return jax.shard_map(
        body,
        mesh=mesh,
        in_specs=(
            P("date", None, "tile", None),
            P("tile", None, None, None),
            P("tile", None, None, None),
            P("tile", None),
            P("tile", None),
            P("tile", None),
            P(None, "tile"),
            P(),
        ),
        out_specs=P(None, None, "tile", "date"),
        check_vma=False,
    )
```

```python
import functools

import jax
import jax.numpy as jnp
from jax import lax
from jax.experimental import pallas as pl
from jax.experimental.pallas import tpu as pltpu
from jax.sharding import PartitionSpec as P

MESH = pl.DeviceIdType.MESH
ROWS = 64


def log(size):
    assert size & (size - 1) == 0
    return size.bit_length() - 1


def kernel(dims, tgt_hbm, roff_hbm, coff_hbm, mask_hbm, smoother_hbm, cx_hbm, cy_hbm, g_hbm, out_ref, divisor_ref,
           tgt, roff, coff, mask, smoother, weights, cx_ref, cy_ref, small_sem, g, rx, ymat, parts, part, recv, final,
           g_sem, send1, recv1, send2, recv2):
    nt, nq, slots, tile_rows, tile_cols, taps, grid_rows, grid_cols, group, rpq, steps, all_dates, bands = dims
    diag, far, side, near, home = range(5)
    tile = lax.axis_index("tile")
    date = lax.axis_index("date")
    turn = 1 - 2 * (tile % 2)
    partner = tile + turn
    ahead = tile - 2 * turn
    behind = tile + 2 * turn
    has_ahead = jnp.logical_and(ahead >= 0, ahead < nt)
    has_behind = jnp.logical_and(behind >= 0, behind < nt)

    def tile_of(slot):
        aim = jnp.where(slot == diag, tile - turn, tile)
        aim = jnp.where(slot == far, ahead, aim)
        aim = jnp.where(slot == side, partner, aim)
        return jnp.where(slot == near, behind, aim)

    def fetch(step):
        return pltpu.make_async_copy(g_hbm.at[pl.ds(2 * step, 2)], g.at[pl.ds(2 * step, 2)], g_sem.at[step])

    pairs = [(tgt_hbm, tgt), (roff_hbm, roff), (coff_hbm, coff), (cy_hbm, cy_ref), (cx_hbm, cx_ref),
             (mask_hbm, mask), (smoother_hbm, smoother)]
    small = [pltpu.make_async_copy(src, dst, small_sem.at[i]) for i, (src, dst) in enumerate(pairs)]
    for copy in small:
        copy.start()
    for step in range(steps):
        fetch(step).start()

    barrier = pltpu.get_barrier_semaphore()
    pl.semaphore_signal(barrier, inc=1, device_id=(date, partner), device_id_type=MESH)
    for c in range(1, nq):
        pl.semaphore_signal(barrier, inc=1, device_id=(lax.rem(date + c, nq), tile), device_id_type=MESH)

    @pl.when(has_ahead)
    def _():
        pl.semaphore_signal(barrier, inc=1, device_id=(date, ahead), device_id_type=MESH)

    @pl.when(has_behind)
    def _():
        pl.semaphore_signal(barrier, inc=1, device_id=(date, behind), device_id_type=MESH)

    m_count, c_count = slots * tile_rows * group, group * grid_rows
    per_slot = tile_rows * group
    m_e = lax.broadcasted_iota(jnp.int32, (m_count, slots * tile_rows), 0)
    n_e = lax.broadcasted_iota(jnp.int32, (m_count, slots * tile_rows), 1)

    def row_of(m):
        return ((m & (per_slot - 1)) >> log(group * rpq)) * rpq + (m & (rpq - 1))

    same_row = row_of(m_e) == (n_e & (tile_rows - 1))
    slot_e = n_e >> log(tile_rows)
    wanted_e = tile_of(m_e >> log(per_slot))
    m = lax.broadcasted_iota(jnp.int32, (m_count, c_count), 0)
    c = lax.broadcasted_iota(jnp.int32, (m_count, c_count), 1)
    wanted = tile_of(m >> log(per_slot))
    band_c = jnp.zeros_like(c)
    for b in range(1, group):
        band_c = jnp.where(c >= b * grid_rows, b, band_c)
    base = c - band_c * grid_rows - 2 * row_of(m)
    base = jnp.where(((m >> log(rpq)) & (group - 1)) == band_c, base, -1)
    for copy in small:
        copy.wait()
    aimed = jnp.full_like(n_e, -1)
    for k in range(slots):
        aimed = jnp.where(slot_e == k, tgt[0, k], aimed)
    pick = jnp.where(jnp.logical_and(same_row, aimed == wanted_e), 1.0, 0.0)
    cy = jnp.dot(pick.astype(jnp.bfloat16), cy_ref[...], preferred_element_type=jnp.float32)
    shift = jnp.zeros_like(m)
    for k in range(slots):
        shift = jnp.where(wanted == tgt[0, k], roff[0, k], shift)
    tap = base - shift
    acc = jnp.zeros((m_count, c_count), jnp.float32)
    for t in range(taps):
        acc = jnp.where(tap == t, cy[:, t:t + 1], acc)
    ymat[...] = acc.astype(jnp.bfloat16)

    def build(r, carry):
        want = tile_of(r)
        coef = jnp.zeros((taps, tile_cols), jnp.float32)
        off = jnp.int32(0)
        for k in range(slots):
            hit = tgt[0, k] == want
            coef = coef + cx_ref[k].astype(jnp.float32) * jnp.where(hit, 1.0, 0.0)
            off = off + jnp.where(hit, coff[0, k], 0)
        row = lax.broadcasted_iota(jnp.int32, (ROWS, tile_cols), 0)
        lane = lax.broadcasted_iota(jnp.int32, (ROWS, tile_cols), 1)
        base = row - 2 * lane - off
        for j in range(grid_cols // ROWS):
            tap = base + j * ROWS
            acc = jnp.zeros((ROWS, tile_cols), jnp.float32)
            for t in range(taps):
                acc = jnp.where(tap == t, coef[t:t + 1, :], acc)
            rx[r, j * ROWS:(j + 1) * ROWS, :] = acc.astype(jnp.bfloat16)
        return carry

    def y_pass(first, count, step):
        rows = ymat[first * per_slot:(first + count) * per_slot, :]
        pair = [
            jnp.dot(rows, g[2 * step + h], preferred_element_type=jnp.float32).reshape(count * nq, 1, 8, grid_cols)
            for h in range(2)
        ]
        both = jnp.concatenate(pair, 1).reshape(count, nq, 16, grid_cols)
        top = both.astype(jnp.bfloat16)
        parts[first:first + count, :, 0, step * 16:(step + 1) * 16, :] = top
        parts[first:first + count, :, 1, step * 16:(step + 1) * 16, :] = (both - top.astype(jnp.float32)).astype(jnp.bfloat16)

    def x_pass(slot, q):
        block = part.shape[2]
        both = jnp.dot(parts[slot, q].reshape(2 * block, grid_cols), rx[slot], preferred_element_type=jnp.float32)
        part[slot, q] = both[:block] + both[block:]

    order = [nq // 2] + [s for s in range(1, nq) if s != nq // 2] + [0]
    blocks = [lax.rem(date + s, nq) for s in order]

    def to_tile(slot, i):
        to = {diag: partner if i % 2 else ahead, far: ahead, side: partner, near: behind}[slot]
        q = blocks[i]
        return pltpu.make_async_remote_copy(
            src_ref=part.at[slot, q], dst_ref=recv.at[slot, q], send_sem=send1.at[slot, q], recv_sem=recv1.at[slot, q],
            device_id=(date, to), device_id_type=MESH)

    def to_date(q):
        return pltpu.make_async_remote_copy(
            src_ref=part.at[home, q], dst_ref=final.at[date], send_sem=send2.at[q], recv_sem=recv2.at[date],
            device_id=(q, tile), device_id_type=MESH)

    def from_date(q):
        return pltpu.make_async_remote_copy(
            src_ref=part.at[home, q], dst_ref=final.at[q], send_sem=send2.at[q], recv_sem=recv2.at[q],
            device_id=(q, tile), device_id_type=MESH)

    build(diag, 0)
    for step in range(steps):
        fetch(step).wait()
    for step in range(steps):
        y_pass(diag, 1, step)
    peers = nq + jnp.where(has_ahead, 1, 0) + jnp.where(has_behind, 1, 0)
    pl.semaphore_wait(barrier, peers)
    for i in range(nq):
        x_pass(diag, blocks[i])

        @pl.when(has_ahead)
        def _(i=i):
            to_tile(diag, i).start()

    lax.fori_loop(1, slots, build, 0)
    for step in range(steps):
        y_pass(far, slots - 1, step)

    for i in range(nq):
        q = blocks[i]
        x_pass(far, q)

        @pl.when(has_ahead)
        def _(i=i):
            to_tile(far, i).start()

        x_pass(side, q)
        if i % 2:
            to_tile(side, i).start()
        x_pass(near, q)
        if i % 2 == 0:

            @pl.when(has_behind)
            def _(i=i):
                to_tile(near, i).start()

        x_pass(home, q)
        joined = near if i % 2 else side

        @pl.when(has_behind)
        def _(i=i, q=q, joined=joined):
            to_tile(diag, i).wait_recv()
            part[joined, q] = part[joined, q] + recv[diag, q]
            if joined == near:
                to_tile(near, i).start()

        if joined == side:
            to_tile(side, i).start()

    def collect(i):
        q = blocks[i]
        to_tile(side, i).wait_recv()
        part[home, q] = part[home, q] + recv[side, q]

        @pl.when(has_behind)
        def _():
            to_tile(far, i).wait_recv()
            part[home, q] = part[home, q] + recv[far, q]

        @pl.when(has_ahead)
        def _():
            to_tile(near, i).wait_recv()
            part[home, q] = part[home, q] + recv[near, q]

    def weigh(t, carry):
        divisor = jnp.float32(0.0)
        for s in range(all_dates):
            w = smoother[t, s] * mask[0, s].astype(jnp.float32)
            weights[t, s] = w
            divisor = divisor + w
        divisor_ref[pl.ds(t, 1), :] = jnp.full((1, tile_cols), divisor, jnp.float32)
        return carry

    lax.fori_loop(0, all_dates, weigh, 0)

    for i in range(nq - 1):
        collect(i)
        to_date(blocks[i]).start()

    rows = bands * rpq
    here = all_dates // nq

    def smooth(source, q, first):
        held = [source[s * rows:(s + 1) * rows, :] for s in range(here)]

        def one(t, carry):
            total = held[0] * weights[t, q * here]
            for s in range(1, here):
                total = total + held[s] * weights[t, q * here + s]
            out_ref[t] = total if first else out_ref[t] + total
            return carry

        lax.fori_loop(0, all_dates, one, 0, unroll=4)

    coming = sorted(order[:-1], key=lambda s: order.index(nq - s))
    for n, s in enumerate(coming[:-1]):
        q = lax.rem(date + s, nq)
        from_date(q).wait_recv()
        smooth(final.at[q], q, n == 0)
    collect(nq - 1)
    smooth(part.at[home, date], date, nq == 2)
    q = lax.rem(date + coming[-1], nq)
    from_date(q).wait_recv()
    smooth(final.at[q], q, False)

    for i in range(nq):
        to_tile(side, i).wait_send()

        @pl.when(has_ahead)
        def _(i=i):
            to_tile(diag, i).wait_send()
            to_tile(far, i).wait_send()

        @pl.when(has_behind)
        def _(i=i):
            to_tile(near, i).wait_send()

    for i in range(nq - 1):
        to_date(blocks[i]).wait_send()


def body(granules, coef_x, coef_y, row_offset, col_offset, targets, mask, smoother):
    dates, bands, grid_rows, grid_cols = granules.shape
    _, slots, tile_cols, taps = coef_x.shape
    tile_rows = coef_y.shape[2]
    nq, nt = lax.axis_size("date"), lax.axis_size("tile")
    rpq = tile_rows // nq
    group = 8 // rpq
    groups = dates * bands // group
    steps = groups // 2
    all_dates = smoother.shape[0]
    dims = (nt, nq, slots, tile_rows, tile_cols, taps, grid_rows, grid_cols, group, rpq, steps, all_dates, bands)
    block = dates * bands * rpq
    vmem = pl.BlockSpec(memory_space=pltpu.VMEM)
    dma = pltpu.SemaphoreType.DMA
    numerator, divisor = pl.pallas_call(
        functools.partial(kernel, dims),
        out_shape=(jax.ShapeDtypeStruct((all_dates, bands * rpq, tile_cols), jnp.float32),
                   jax.ShapeDtypeStruct((all_dates, tile_cols), jnp.float32)),
        in_specs=[pl.BlockSpec(memory_space=pl.ANY)] * 8,
        out_specs=(vmem, vmem),
        scratch_shapes=[
            pltpu.SMEM((1, slots), jnp.int32),
            pltpu.SMEM((1, slots), jnp.int32),
            pltpu.SMEM((1, slots), jnp.int32),
            pltpu.SMEM((1, all_dates), jnp.int32),
            pltpu.SMEM((all_dates, all_dates), jnp.float32),
            pltpu.SMEM((all_dates, all_dates), jnp.float32),
            pltpu.VMEM((slots, taps, tile_cols), jnp.bfloat16),
            pltpu.VMEM((slots * tile_rows, taps), jnp.bfloat16),
            dma((7,)),
            pltpu.VMEM((groups, group * grid_rows, grid_cols), jnp.bfloat16),
            pltpu.VMEM((slots, grid_cols, tile_cols), jnp.bfloat16),
            pltpu.VMEM((slots * tile_rows * group, group * grid_rows), jnp.bfloat16),
            pltpu.VMEM((slots, nq, 2, block, grid_cols), jnp.bfloat16),
            pltpu.VMEM((slots, nq, block, tile_cols), jnp.float32),
            pltpu.VMEM((slots, nq, block, tile_cols), jnp.float32),
            pltpu.VMEM((nq, block, tile_cols), jnp.float32),
            dma((steps,)),
            dma((slots, nq)),
            dma((slots, nq)),
            dma((nq,)),
            dma((nq,)),
        ],
        compiler_params=pltpu.CompilerParams(
            collective_id=0, has_side_effects=True, vmem_limit_bytes=60 * 1024 * 1024),
        cost_estimate=pl.CostEstimate(flops=2_000_000_000, bytes_accessed=4_000_000, transcendentals=0),
    )(targets, row_offset, col_offset, mask.reshape(1, all_dates), smoother,
      jnp.transpose(coef_x[0], (0, 2, 1)), coef_y[0].reshape(slots * tile_rows, taps),
      granules.reshape(groups, group * grid_rows, grid_cols))
    smoothed = numerator / divisor[:, None, :]
    return smoothed.reshape(all_dates, bands, 1, rpq * tile_cols)


def solution(mesh):
    return jax.shard_map(
        body,
        mesh=mesh,
        in_specs=(
            P("date", None, "tile", None),
            P("tile", None, None, None),
            P("tile", None, None, None),
            P("tile", None),
            P("tile", None),
            P("tile", None),
            P(None, "tile"),
            P(),
        ),
        out_specs=P(None, None, "tile", "date"),
        check_vma=False,
    )
```
